32 devices in a mesh: seq: 8 (over z, y), chan: 4 (over x, core).
Axes of the slice: x: 2, y: 2, z: 4, core: 2. Of those that a mesh axis runs over, the one named last changes fastest.
Arguments:
- query_proj: bfloat16 [1024, 4096], P('seq', 'chan'), may hold values from -6 to 6
- key_proj: bfloat16 [1024, 4096], P('seq', 'chan'), may hold values from -6 to 6
- value_proj: bfloat16 [1024, 4096], P('seq', 'chan'), may hold values from -6 to 6
- short_taps: float32 [3, 3, 4096], P(None, None, 'chan'), may hold values from -2.5 to 2.5
- skip_gain: float32 [4096], P('chan'), may hold values from 0.5 to 1.5
- long_filter: float32 [4096, 1024], P(('chan', 'seq')), may hold values from -1024 to 1024
- out_grad: bfloat16 [1024, 4096], P('seq', 'chan'), may hold values from -6 to 6
Outputs:
- mixed_out: bfloat16 [1024, 4096], P('seq', 'chan')
- query_grad: bfloat16 [1024, 4096], P('seq', 'chan')
- key_grad: bfloat16 [1024, 4096], P('seq', 'chan')
- value_grad: bfloat16 [1024, 4096], P('seq', 'chan')
- filter_grad: float32 [4096, 1024], P(('chan', 'seq'))
The draws below stay inside these ranges and needn't reach their ends.
All inputs are finite; a program needn't handle non-finite values.
Results may differ from the reference program's by a relative error of at most 0.0075.
Values may be sent and summed in bfloat16 or wider, within the bound.
A program may use at most 64 MiB of HBM per device.

```python
import math
import jax
import jax.numpy as jnp

MODEL_WIDTH = 4096
SHORT = 3
SEQUENCE_LENGTH = 1024


def draw_long_filter(key, part):
    random_subkeys = jax.random.split(key, 6)
    lag_axis = jnp.arange(SEQUENCE_LENGTH, dtype=jnp.float32)[None, :]
    slow_share = 0.5
    roughness = jax.random.truncated_normal(random_subkeys[0], -4.0, 4.0, (MODEL_WIDTH, SEQUENCE_LENGTH), jnp.float32)
    slow_mask = jax.random.bernoulli(random_subkeys[1], slow_share, (MODEL_WIDTH, 1))
    slow_rate = jnp.exp(jax.random.uniform(random_subkeys[2], (MODEL_WIDTH, 1), jnp.float32, math.log(0.2 / SEQUENCE_LENGTH), math.log(2.0 / SEQUENCE_LENGTH)))
    fast_rate = jnp.exp(jax.random.uniform(random_subkeys[3], (MODEL_WIDTH, 1), jnp.float32, math.log(1.0 / 50.0), math.log(1.0 / 20.0)))
    decay_rate = jnp.where(slow_mask, slow_rate, fast_rate)
    envelope = jnp.exp(-decay_rate * lag_axis)
    for pulse_index in range(3):
        starting_delay = jax.random.randint(jax.random.fold_in(random_subkeys[4], pulse_index), (MODEL_WIDTH, 1), 1, SEQUENCE_LENGTH).astype(jnp.float32)
        multiplier = jax.random.uniform(jax.random.fold_in(random_subkeys[5], pulse_index), (MODEL_WIDTH, 1), jnp.float32, 0.5, 0.8)
        envelope = envelope * jnp.where(lag_axis >= starting_delay, multiplier, 1.0)
    energy = (1.0 - jnp.exp(-2.0 * decay_rate * SEQUENCE_LENGTH)) / (1.0 - jnp.exp(-2.0 * decay_rate))
    return roughness * envelope * (math.sqrt(SEQUENCE_LENGTH) / jnp.sqrt(energy))


def level_of(rng, extent, shards, low, largest):
    gain = 1.0
    for dim, blocks in shards:
        steps = jax.random.uniform(jax.random.fold_in(jax.random.fold_in(rng, 6), dim), (blocks,), jnp.float32, low / len(shards), largest / len(shards))
        gain = gain * jnp.repeat(jnp.exp(steps), extent[dim] // blocks).reshape((-1,) + (1,) * (len(extent) - 1 - dim))
    return gain


def gaussian(key, dims, spread, reach, shards=(), held_as=jnp.bfloat16):
    values = jax.random.normal(key, dims, jnp.float32) * spread
    if len(shards) > 0:
        values = level_of(key, dims, shards, -0.22, 0.18) * values
    return jnp.clip(values, min=-reach, max=reach).astype(held_as)


def setup_inputs(seed: int = 0) -> dict:
    keys = jax.random.split(jax.random.key(seed), 8)
    query_proj = gaussian(keys[0], (SEQUENCE_LENGTH, MODEL_WIDTH), 1.0, 6.0, ((0, 8), (1, 4)))
    key_proj = gaussian(keys[1], (SEQUENCE_LENGTH, MODEL_WIDTH), 1.0, 6.0, ((0, 8), (1, 4)))
    value_proj = gaussian(keys[2], (SEQUENCE_LENGTH, MODEL_WIDTH), 1.0, 6.0, ((0, 8), (1, 4)))
    short_taps = gaussian(keys[3], (3, SHORT, MODEL_WIDTH), 0.6, 2.5, ((2, 4),), jnp.float32)
    skip_gain = jnp.clip(0.5 + 1.0 * jax.random.uniform(keys[4], (MODEL_WIDTH,), jnp.float32) ** level_of(keys[4], (MODEL_WIDTH,), ((0, 4),), -0.2, 0.2), 0.5, 1.5)
    long_filter = draw_long_filter(jax.random.fold_in(keys[7], 71), 0)
    out_grad = gaussian(keys[6], (SEQUENCE_LENGTH, MODEL_WIDTH), 1.0, 6.0, ((0, 8), (1, 4)))
    return {"query_proj": query_proj, "key_proj": key_proj, "value_proj": value_proj, "short_taps": short_taps, "skip_gain": skip_gain, "long_filter": long_filter, "out_grad": out_grad}


def causal_taps(signal, weights):
    length = signal.shape[0]
    padded = jnp.concatenate([jnp.zeros((2, signal.shape[1]), signal.dtype), signal], 0)
    return weights[0] * padded[2:length + 2] + weights[1] * padded[1:length + 1] + weights[2] * padded[0:length]

def trailing_taps(signal, weights):
    length = signal.shape[0]
    padded = jnp.concatenate([signal, jnp.zeros((2, signal.shape[1]), signal.dtype)], 0)
    return weights[0] * padded[0:length] + weights[1] * padded[1:length + 1] + weights[2] * padded[2:length + 2]

def reference(query_proj, key_proj, value_proj, short_taps, skip_gain, long_filter, out_grad):
    length = query_proj.shape[0]
    doubled = 2 * length
    factor_root = 1.0 / math.sqrt(length)
    query_short = causal_taps(query_proj.astype(jnp.float32), short_taps[0]).astype(jnp.bfloat16)
    key_short = causal_taps(key_proj.astype(jnp.float32), short_taps[1]).astype(jnp.bfloat16)
    value_short = causal_taps(value_proj.astype(jnp.float32), short_taps[2]).astype(jnp.bfloat16)
    key_wide = key_short.astype(jnp.float32)
    value_wide = value_short.astype(jnp.float32)
    product_in = (key_wide * value_wide).astype(jnp.bfloat16)
    kernel_own = long_filter.T * factor_root
    kernel_mirror = kernel_own[:, ::-1]
    kernel_full = jnp.concatenate([kernel_own[:1] + kernel_mirror[:1], kernel_own[1:], jnp.zeros_like(kernel_own[:1]), kernel_mirror[1:][::-1]], 0)
    spectrum_kernel = jnp.fft.rfft(kernel_full, axis=0)
    input_wide = product_in.astype(jnp.float32)
    input_spectrum = jnp.fft.rfft(input_wide, n=doubled, axis=0)
    long_mix = (jnp.fft.irfft(spectrum_kernel * input_spectrum, n=doubled, axis=0)[:length] + skip_gain * input_wide).astype(jnp.bfloat16)
    mix_wide = long_mix.astype(jnp.float32)
    query_wide = query_short.astype(jnp.float32)
    mixed_out = (query_wide * mix_wide).astype(jnp.bfloat16)
    grad_wide = out_grad.astype(jnp.float32)
    gate_grad = (grad_wide * query_wide).astype(jnp.bfloat16)
    gate_wide = gate_grad.astype(jnp.float32)
    spectrum_grad = jnp.fft.rfft(gate_wide, n=doubled, axis=0)
    input_grad = (jnp.fft.irfft(jnp.conj(spectrum_kernel) * spectrum_grad, n=doubled, axis=0)[:length] + skip_gain * gate_wide).astype(jnp.bfloat16)
    lagged = jnp.fft.irfft(jnp.conj(input_spectrum) * spectrum_grad, n=doubled, axis=0)
    reversed_part = jnp.concatenate([lagged[:1], lagged[length + 1:][::-1]], 0)
    filter_grad = ((lagged[:length] + reversed_part[:, ::-1]) * factor_root).T
    input_back = input_grad.astype(jnp.float32)
    query_grad = trailing_taps(grad_wide * mix_wide, short_taps[0]).astype(jnp.bfloat16)
    key_grad = trailing_taps(input_back * value_wide, short_taps[1]).astype(jnp.bfloat16)
    value_grad = trailing_taps(input_back * key_wide, short_taps[2]).astype(jnp.bfloat16)
    return (mixed_out, query_grad, key_grad, value_grad, filter_grad)
```

```python
import functools
import math

import jax
import jax.numpy as jnp
import ml_dtypes
import numpy as np
from jax import lax
from jax.experimental import pallas as pl
from jax.experimental.pallas import tpu as pltpu
from jax.sharding import PartitionSpec as P

F32 = jnp.float32
BF16 = jnp.bfloat16
BLOCK = 128


def transform_tables(length):
    odd = 2 * np.arange(length, dtype=np.int64) + 1
    counts = odd[:, None] * np.arange(length, dtype=np.int64)[None, :] % (4 * length)
    angles = counts * (math.pi / (2 * length))
    forward = np.concatenate([np.cos(angles), np.sin(angles)], 0)
    forward = forward.astype(ml_dtypes.bfloat16)
    return forward, np.ascontiguousarray(forward.T)


def dense_kernel(
    n_seq,
    n_chan,
    query_ref,
    key_ref,
    value_ref,
    taps_ref,
    skip_ref,
    filter_ref,
    cotangent_ref,
    forward_hbm,
    inverse_hbm,
    mixed_ref,
    query_grad_ref,
    key_grad_ref,
    value_grad_ref,
    filter_grad_ref,
    forward,
    inverse,
    extended,
    shorted,
    gated,
    halo_out,
    halo_in,
    block_out,
    block_in,
    result_out,
    result_in,
    filter_out,
    filter_in,
    skip_in,
    terms_out,
    terms_in,
    spectra,
    products,
    even_part,
    odd_part,
    lag_spectra,
    halo_sent,
    halo_got,
    block_sent,
    block_got,
    result_sent,
    result_got,
    single_sent,
    single_got,
    table_got,
):
    rows = query_ref.shape[0]
    length = filter_ref.shape[1]
    chunk = 2 * rows
    chunks = length // chunk
    me = lax.axis_index("seq")
    chan = lax.axis_index("chan")
    is_owner = chan % 2 == 0
    not_owner = chan % 2 == 1
    owner_chan = jnp.where(is_owner, chan, n_chan - 1 - chan)
    other_chan = n_chan - 1 - owner_chan
    side = chan % 2
    mirrored_seq = n_seq - 1 - me

    def device(seq, chan_index):
        return {"seq": seq, "chan": chan_index}

    def remote(source, target, sent, got, where):
        return pltpu.make_async_remote_copy(
            src_ref=source,
            dst_ref=target,
            send_sem=sent,
            recv_sem=got,
            device_id=where,
            device_id_type=pl.DeviceIdType.MESH,
        )

    def await_on(buffer, semaphore):
        pltpu.make_async_copy(buffer, buffer, semaphore).wait()

    def lanes_of(block):
        return pl.ds(pl.multiple_of(block * BLOCK, BLOCK), BLOCK)

    forward_copy = pltpu.make_async_copy(forward_hbm, forward, table_got.at[0])
    inverse_copy = pltpu.make_async_copy(inverse_hbm, inverse, table_got.at[1])

    barrier = pltpu.get_barrier_semaphore()

    def greet(index, carry):
        seq = index % n_seq
        target = jnp.where(index < n_seq, owner_chan, other_chan)

        @pl.when(jnp.logical_or(seq != me, target != chan))
        def _():
            pl.semaphore_signal(
                barrier,
                inc=1,
                device_id=device(seq, target),
                device_id_type=pl.DeviceIdType.MESH,
            )

        return carry

    lax.fori_loop(0, 2 * n_seq, greet, 0)

    @pl.when(is_owner)
    def _():
        forward_copy.start()
        inverse_copy.start()

    sources = (query_ref, key_ref, value_ref)
    for p in range(3):
        extended[p, 8 : rows + 8, :] = sources[p][...].astype(F32)
    extended[3, 8 : rows + 8, :] = cotangent_ref[...].astype(F32)
    halo_out[0] = jnp.concatenate([extended[p, rows + 6 : rows + 8, :] for p in range(4)], 0)
    halo_out[1] = jnp.concatenate([extended[p, 8:10, :] for p in range(4)], 0)

    pl.semaphore_wait(barrier, 2 * n_seq - 1)

    to_next = remote(
        halo_out.at[0],
        halo_in.at[0],
        halo_sent.at[0],
        halo_got.at[0],
        device(jnp.minimum(me + 1, n_seq - 1), chan),
    )
    to_previous = remote(
        halo_out.at[1],
        halo_in.at[1],
        halo_sent.at[1],
        halo_got.at[1],
        device(jnp.maximum(me - 1, 0), chan),
    )

    @pl.when(me < n_seq - 1)
    def _():
        to_next.start()

    @pl.when(me > 0)
    def _():
        to_previous.start()

    @pl.when(not_owner)
    def _():
        filter_out[...] = filter_ref[...].astype(BF16)

    @pl.when(me > 0)
    def _():
        await_on(halo_in.at[0], halo_got.at[0])

    @pl.when(me == 0)
    def _():
        halo_in[0] = jnp.zeros(halo_in.shape[1:], F32)

    @pl.when(me < n_seq - 1)
    def _():
        await_on(halo_in.at[1], halo_got.at[1])

    @pl.when(me == n_seq - 1)
    def _():
        halo_in[1] = jnp.zeros(halo_in.shape[1:], F32)

    for p in range(4):
        extended[p, 6:8, :] = halo_in[0, 2 * p : 2 * p + 2, :]
        extended[p, rows + 8 : rows + 16, :] = jnp.concatenate(
            [halo_in[1, 2 * p : 2 * p + 2, :], jnp.zeros((6, halo_in.shape[2]), F32)], 0
        )

    def owner_of(block):
        return jnp.where(is_owner, block, n_seq - 1 - block)

    def send_block(step, carry):
        block = (me + n_seq // 2 + step) % n_seq
        lanes = lanes_of(block)
        for p in range(3):
            total = taps_ref[p, 0:1, lanes] * extended[p, 8 : rows + 16, lanes]
            total += taps_ref[p, 1:2, lanes] * extended[p, 7 : rows + 15, lanes]
            total += taps_ref[p, 2:3, lanes] * extended[p, 6 : rows + 14, lanes]
            shorted[p, :, lanes] = total.astype(BF16).astype(F32)
        product = shorted[1, 0:rows, lanes] * shorted[2, 0:rows, lanes]
        block_out[block, 0:rows, :] = product.astype(BF16)
        gate = extended[3, 8 : rows + 8, lanes] * shorted[0, 0:rows, lanes]
        block_out[block, rows : 2 * rows, :] = gate.astype(BF16)
        target = owner_of(block)
        here = jnp.logical_and(is_owner, block == me)

        @pl.when(here)
        def _():
            pltpu.make_async_copy(
                block_out.at[block], block_in.at[0, me], block_got.at[0, me]
            ).start()

        @pl.when(jnp.logical_not(here))
        def _():
            remote(
                block_out.at[block],
                block_in.at[side, me],
                block_sent.at[block],
                block_got.at[side, me],
                device(target, owner_chan),
            ).start()

        return carry

    lax.fori_loop(0, n_seq, send_block, 0)

    filter_copy = remote(
        filter_out,
        filter_in,
        single_sent.at[0],
        single_got.at[0],
        device(mirrored_seq, owner_chan),
    )
    skip_copy = remote(
        skip_ref, skip_in, single_sent.at[1], single_got.at[1], device(mirrored_seq, owner_chan)
    )
    terms_copy = remote(
        terms_out, terms_in, single_sent.at[2], single_got.at[2], device(mirrored_seq, other_chan)
    )

    @pl.when(not_owner)
    def _():
        skip_copy.start()
        filter_copy.start()

    def columns_of(seq):
        return jnp.concatenate(
            [
                block_in[0, seq, 0:rows, :],
                block_in[1, seq, 0:rows, :],
                block_in[0, seq, rows : 2 * rows, :],
                block_in[1, seq, rows : 2 * rows, :],
            ],
            1,
        )

    wide = 2 * BLOCK

    @pl.when(is_owner)
    def _():
        forward_copy.wait()
        for step in range(chunks):
            piece = (me // 2 + step) % chunks
            for half in range(2):
                for from_side in range(2):
                    seq = 2 * piece + half
                    await_on(block_in.at[from_side, seq], block_got.at[from_side, seq])
            columns = jnp.concatenate([columns_of(2 * piece), columns_of(2 * piece + 1)], 0)
            lags = pl.ds(pl.multiple_of(piece * chunk, chunk), chunk)

            def transform(index, carry):
                at = pl.ds(pl.multiple_of(index * chunk, chunk), chunk)
                term = jnp.dot(forward[at, lags], columns, preferred_element_type=F32)
                if step == 0:
                    spectra[at, :] = term
                else:
                    spectra[at, :] += term
                return carry

            lax.fori_loop(0, 2 * chunks, transform, 0)

        down = lax.broadcasted_iota(jnp.int32, (BLOCK, BLOCK), 0)
        across = lax.broadcasted_iota(jnp.int32, (BLOCK, BLOCK), 1)
        flip = jnp.where(down + across == BLOCK - 1, 1.0, 0.0).astype(BF16)

        def flipped(values):
            return jnp.dot(flip, values, preferred_element_type=F32)

        def halves(index):
            start = pl.multiple_of(index * chunk, chunk)
            return pl.ds(start, chunk), pl.ds(length + start, chunk)

        def lag_products(index, carry):
            first, second = halves(index)
            input_cos, input_sin = spectra[first, 0:wide], spectra[second, 0:wide]
            grad_cos, grad_sin = spectra[first, wide:], spectra[second, wide:]
            real = input_cos * grad_cos + input_sin * grad_sin
            imag = input_sin * grad_cos - input_cos * grad_sin
            lag_spectra[:, first] = real.T.astype(BF16)
            lag_spectra[:, second] = imag.T.astype(BF16)
            return carry

        lax.fori_loop(0, chunks, lag_products, 0)
        scale = 1.0 / (length * math.sqrt(length))

        def filter_terms(index, carry):
            lags = pl.ds(pl.multiple_of(index * chunk, chunk), chunk)
            cosine = jnp.dot(
                lag_spectra[:, 0:length], forward[0:length, lags], preferred_element_type=F32
            )
            sine = jnp.dot(
                lag_spectra[:, length:], forward[length:, lags], preferred_element_type=F32
            )
            ahead = cosine - sine
            behind = (cosine + sine).astype(BF16)
            terms_out[:, lags] = ((ahead[BLOCK:] + flipped(behind[:BLOCK])) * scale).astype(BF16)
            filter_grad_ref[:, lags] = (ahead[:BLOCK] + flipped(behind[BLOCK:])) * scale
            return carry

        lax.fori_loop(0, chunks, filter_terms, 0)
        terms_copy.start()

        await_on(filter_in, single_got.at[0])
        own = filter_ref[...]
        other = filter_in[...]
        own_flipped = flipped(own.astype(BF16))
        other_flipped = flipped(other)
        other = other.astype(F32)
        even_part[0:BLOCK, :] = (own + other_flipped).astype(BF16)
        even_part[BLOCK:, :] = (other + own_flipped).astype(BF16)
        odd_part[0:BLOCK, :] = (own - other_flipped).astype(BF16)
        odd_part[BLOCK:, :] = (other - own_flipped).astype(BF16)

        def spectral_products(index, carry):
            first, second = halves(index)
            contracted = (((1,), (1,)), ((), ()))
            kernel_cos = lax.dot_general(
                forward[first, :], even_part[...], contracted, preferred_element_type=F32
            )
            kernel_sin = lax.dot_general(
                forward[second, :], odd_part[...], contracted, preferred_element_type=F32
            )
            input_cos, input_sin = spectra[first, 0:wide], spectra[second, 0:wide]
            grad_cos, grad_sin = spectra[first, wide:], spectra[second, wide:]
            mix_cos = kernel_cos * input_cos - kernel_sin * input_sin
            mix_sin = kernel_cos * input_sin + kernel_sin * input_cos
            back_cos = kernel_cos * grad_cos + kernel_sin * grad_sin
            back_sin = kernel_cos * grad_sin - kernel_sin * grad_cos
            products[first, 0:wide] = mix_cos.astype(BF16)
            products[second, 0:wide] = mix_sin.astype(BF16)
            products[first, wide:] = back_cos.astype(BF16)
            products[second, wide:] = back_sin.astype(BF16)
            return carry

        lax.fori_loop(0, chunks, spectral_products, 0)
        await_on(skip_in, single_got.at[1])
        gains = [skip_ref[pl.ds(me, 1), :], skip_in[pl.ds(mirrored_seq, 1), :]]
        gains = jnp.concatenate(gains + gains, 1)
        inverse_copy.wait()

        def results(index, carry):
            at = pl.ds(pl.multiple_of(index * chunk, chunk), chunk)
            sums = jnp.dot(inverse[at, :], products[...], preferred_element_type=F32) * scale
            for half in range(2):
                seq = 2 * index + half
                here = sums[half * rows : (half + 1) * rows]
                here = here + gains * columns_of(seq).astype(F32)
                before = (seq + n_seq - 1) % n_seq
                kept = jnp.where(seq > 0, 1.0, 0.0)
                for to_side in range(2):
                    mix = here[:, to_side * BLOCK : (to_side + 1) * BLOCK]
                    back = here[:, wide + to_side * BLOCK : wide + (to_side + 1) * BLOCK]
                    result_out[to_side, seq, 0:rows, :] = mix.astype(BF16)
                    result_out[to_side, seq, rows : 2 * rows, :] = back.astype(BF16)
                    edge = jnp.concatenate([mix[0:2], back[0:2], jnp.zeros((12, BLOCK), F32)], 0)
                    result_out[to_side, before, 2 * rows :, :] = (edge * kept).astype(BF16)
            return carry

        lax.fori_loop(0, chunks, results, 0)

        def send_result(step, carry):
            seq = (me + n_seq // 2 + step) % n_seq

            remote(
                result_out.at[1, seq],
                result_in.at[mirrored_seq],
                result_sent.at[1, seq],
                result_got.at[mirrored_seq],
                device(seq, other_chan),
            ).start()

            @pl.when(seq == me)
            def _():
                pltpu.make_async_copy(
                    result_out.at[0, me], result_in.at[me], result_got.at[me]
                ).start()

            @pl.when(seq != me)
            def _():
                remote(
                    result_out.at[0, seq],
                    result_in.at[me],
                    result_sent.at[0, seq],
                    result_got.at[me],
                    device(seq, owner_chan),
                ).start()

            return carry

        lax.fori_loop(0, n_seq, send_result, 0)

    def finish_block(step, carry):
        source = (me + n_seq // 2 + n_seq - step) % n_seq
        block = owner_of(source)
        lanes = lanes_of(block)
        await_on(result_in.at[block], result_got.at[block])
        edge = result_in[block, 2 * rows :, :].astype(F32)
        mix = result_in[block, 0:rows, :].astype(F32)
        back = result_in[block, rows : 2 * rows, :].astype(F32)
        spare = jnp.zeros((6, BLOCK), F32)
        mixed_ref[:, lanes] = (shorted[0, 0:rows, lanes] * mix).astype(BF16)
        mix = jnp.concatenate([mix, edge[0:2], spare], 0)
        back = jnp.concatenate([back, edge[2:4], spare], 0)
        gated[0] = extended[3, 8 : rows + 16, lanes] * mix
        gated[1] = back * shorted[2, :, lanes]
        gated[2] = back * shorted[1, :, lanes]
        for p, target in enumerate((query_grad_ref, key_grad_ref, value_grad_ref)):
            total = taps_ref[p, 0:1, lanes] * gated[p, 0:rows, :]
            total += taps_ref[p, 1:2, lanes] * gated[p, 1 : rows + 1, :]
            total += taps_ref[p, 2:3, lanes] * gated[p, 2 : rows + 2, :]
            target[:, lanes] = total.astype(BF16)
        return carry

    lax.fori_loop(0, n_seq, finish_block, 0)

    @pl.when(not_owner)
    def _():
        await_on(terms_in, single_got.at[2])
        filter_grad_ref[...] = terms_in[...].astype(F32)
        filter_copy.wait_send()
        skip_copy.wait_send()

    @pl.when(me < n_seq - 1)
    def _():
        to_next.wait_send()

    @pl.when(me > 0)
    def _():
        to_previous.wait_send()

    def drain_block(block, carry):
        @pl.when(jnp.logical_or(not_owner, block != me))
        def _():
            await_on(block_out.at[block], block_sent.at[block])

        return carry

    lax.fori_loop(0, n_seq, drain_block, 0)

    @pl.when(is_owner)
    def _():
        terms_copy.wait_send()

        def drain_result(seq, carry):
            await_on(result_out.at[1, seq], result_sent.at[1, seq])

            @pl.when(seq != me)
            def _():
                await_on(result_out.at[0, seq], result_sent.at[0, seq])

            return carry

        lax.fori_loop(0, n_seq, drain_result, 0)


def dense_device(
    n_seq, n_chan, tables, query, key, value, short_taps, skip_gain, long_filter, cotangent
):
    rows, width = query.shape
    channels, length = long_filter.shape
    whole = pl.BlockSpec(memory_space=pltpu.VMEM)
    apart = pl.BlockSpec(memory_space=pl.ANY)
    sequence_like = jax.ShapeDtypeStruct((rows, width), BF16)
    wide = 2 * channels
    semaphores = pltpu.SemaphoreType.DMA
    return pl.pallas_call(
        functools.partial(dense_kernel, n_seq, n_chan),
        out_shape=(sequence_like,) * 4 + (jax.ShapeDtypeStruct((channels, length), F32),),
        in_specs=[whole] * 7 + [apart] * 2,
        out_specs=(whole,) * 5,
        scratch_shapes=[
            pltpu.VMEM((2 * length, length), BF16),
            pltpu.VMEM((length, 2 * length), BF16),
            pltpu.VMEM((4, rows + 16, width), F32),
            pltpu.VMEM((3, rows + 8, width), F32),
            pltpu.VMEM((3, rows + 8, channels), F32),
            pltpu.VMEM((2, 8, width), F32),
            pltpu.VMEM((2, 8, width), F32),
            pltpu.VMEM((n_seq, 2 * rows, channels), BF16),
            pltpu.VMEM((2, n_seq, 2 * rows, channels), BF16),
            pltpu.VMEM((2, n_seq, 2 * rows + 16, channels), BF16),
            pltpu.VMEM((n_seq, 2 * rows + 16, channels), BF16),
            pltpu.VMEM((channels, length), BF16),
            pltpu.VMEM((channels, length), BF16),
            pltpu.VMEM((n_seq, channels), F32),
            pltpu.VMEM((channels, length), BF16),
            pltpu.VMEM((channels, length), BF16),
            pltpu.VMEM((2 * length, 2 * wide), F32),
            pltpu.VMEM((2 * length, 2 * wide), BF16),
            pltpu.VMEM((wide, length), BF16),
            pltpu.VMEM((wide, length), BF16),
            pltpu.VMEM((wide, 2 * length), BF16),
            semaphores((2,)),
            semaphores((2,)),
            semaphores((n_seq,)),
            semaphores((2, n_seq)),
            semaphores((2, n_seq)),
            semaphores((n_seq,)),
            semaphores((3,)),
            semaphores((3,)),
            semaphores((2,)),
        ],
        compiler_params=pltpu.CompilerParams(
            collective_id=0, has_side_effects=True, vmem_limit_bytes=56 * 1024 * 1024
        ),
    )(
        query,
        key,
        value,
        short_taps,
        skip_gain.reshape(n_seq, channels),
        long_filter,
        cotangent,
        *[jnp.asarray(table) for table in tables],
    )


exact_mode = lax.Precision.HIGHEST


def from_partner(array, axis, stride):
    return lax.ppermute(array, axis, [(i, i ^ 1 << stride) for i in range(lax.axis_size(axis))])


def passed_along(array, axis, by):
    length = lax.axis_size(axis)
    pairs = [(i, i + by) for i in range(length) if 0 <= i + by < length]
    return lax.ppermute(array, axis, pairs)


def divisor_pair(total_size):
    first_side = 1
    for candidate in range(1, math.isqrt(total_size) + 1):
        if total_size % candidate == 0:
            first_side = candidate
    return (first_side, total_size // first_side)


def angle_table(height, across, period):
    counts = (
        jnp.arange(height, dtype=jnp.int32)[:, None]
        * jnp.arange(across, dtype=jnp.int32)[None, :]
        % period
    )
    angles = counts.astype(jnp.float32) * (2.0 * math.pi / period)
    return (jnp.cos(angles), jnp.sin(angles))


def make_tables(total_size):
    first_side, second_side = divisor_pair(total_size)
    return (
        angle_table(first_side, first_side, first_side),
        angle_table(first_side, second_side, total_size),
        angle_table(second_side, second_side, second_side),
        first_side,
        second_side,
    )


def right_product(values, matrix):
    return jnp.einsum("ckm,ml->ckl", values, matrix, precision=exact_mode)


def left_product(matrix, values):
    return jnp.einsum("kn,cnm->ckm", matrix, values, precision=exact_mode)


def spectrum_of(signal, tables):
    (
        (cos_first, sin_first),
        (cosine_rotation, sin_twist),
        (cos_second, sin_second),
        first_side,
        second_side,
    ) = tables
    shaped = signal.reshape(signal.shape[0], first_side, second_side)
    section_real = left_product(cos_first, shaped)
    section_imag = -left_product(sin_first, shaped)
    twist_real = section_real * cosine_rotation + section_imag * sin_twist
    twist_imag = section_imag * cosine_rotation - section_real * sin_twist
    return (
        right_product(twist_real, cos_second) + right_product(twist_imag, sin_second),
        right_product(twist_imag, cos_second) - right_product(twist_real, sin_second),
    )


def signal_of(spectrum, tables):
    (
        (cos_first, sin_first),
        (cosine_rotation, sin_twist),
        (cos_second, sin_second),
        first_side,
        second_side,
    ) = tables
    spec_real, spec_imag = spectrum
    section_real = right_product(spec_real, cos_second) - right_product(spec_imag, sin_second)
    section_imag = right_product(spec_imag, cos_second) + right_product(spec_real, sin_second)
    twist_real = section_real * cosine_rotation - section_imag * sin_twist
    twist_imag = section_imag * cosine_rotation + section_real * sin_twist
    result = left_product(cos_first, twist_real) - left_product(sin_first, twist_imag)
    return result.reshape(result.shape[0], -1) / (first_side * second_side)


def times_spec(former, latter):
    return (
        former[0] * latter[0] - former[1] * latter[1],
        former[0] * latter[1] + former[1] * latter[0],
    )


def conj_times(former, latter):
    return (
        former[0] * latter[0] + former[1] * latter[1],
        former[0] * latter[1] - former[1] * latter[0],
    )


def mirror_rows(block_rows):
    mirrored = block_rows
    for bit_index in range((lax.axis_size("seq") * lax.axis_size("chan")).bit_length() - 1):
        mirrored = from_partner(mirrored, ("seq", "chan"), bit_index)
    return mirrored[::-1]


def per_device(query_proj, key_proj, value_proj, short_taps, skip_gain, long_filter, out_grad):
    positions = query_proj.shape[0]
    channels, length = long_filter.shape
    doubled = 2 * length
    factor_root = 1.0 / math.sqrt(length)
    tables = make_tables(doubled)
    own_skip = lax.dynamic_slice_in_dim(skip_gain, lax.axis_index("seq") * channels, channels)[
        :, None
    ]
    stacked = jnp.stack([query_proj, key_proj, value_proj])
    previous = passed_along(stacked[:, positions - 2 :], "seq", 1)
    extended = jnp.concatenate([previous, stacked], 1).astype(jnp.float32)
    tap_rows = short_taps[:, :, None, :]
    shorted = (
        tap_rows[:, 0] * extended[:, 2 : positions + 2]
        + tap_rows[:, 1] * extended[:, 1 : positions + 1]
        + tap_rows[:, 2] * extended[:, 0:positions]
    )
    shorted = shorted.astype(jnp.bfloat16)
    query_short, key_short, value_short = (shorted[0], shorted[1], shorted[2])
    key_wide = key_short.astype(jnp.float32)
    value_wide = value_short.astype(jnp.float32)
    product_in = (key_wide * value_wide).astype(jnp.bfloat16)
    kernel_own = long_filter * factor_root
    kernel_mirror = mirror_rows(kernel_own)
    zero_column = jnp.zeros((channels, 1), jnp.float32)
    kernel_full = jnp.concatenate(
        [
            kernel_own[:, :1] + kernel_mirror[:, :1],
            kernel_own[:, 1:],
            zero_column,
            kernel_mirror[:, 1:][:, ::-1],
        ],
        1,
    )
    spectrum_kernel = spectrum_of(kernel_full, tables)
    query_wide = query_short.astype(jnp.float32)
    chan_product = lax.all_to_all(product_in.T, "seq", split_axis=0, concat_axis=1, tiled=True)
    input_wide = chan_product.astype(jnp.float32)
    input_spectrum = spectrum_of(
        jnp.concatenate([input_wide, jnp.zeros_like(input_wide)], 1), tables
    )
    mixed_wide = signal_of(times_spec(spectrum_kernel, input_spectrum), tables)[:, :length]
    chan_mix, input_spectrum = (
        (mixed_wide + own_skip * input_wide).astype(jnp.bfloat16),
        input_spectrum,
    )
    long_mix = lax.all_to_all(chan_mix, "seq", split_axis=1, concat_axis=0, tiled=True).T
    gate_grad = (out_grad.astype(jnp.float32) * query_wide).astype(jnp.bfloat16)
    chan_gate = lax.all_to_all(gate_grad.T, "seq", split_axis=0, concat_axis=1, tiled=True)
    grad_wide = chan_gate.astype(jnp.float32)
    spectrum_grad = spectrum_of(jnp.concatenate([grad_wide, jnp.zeros_like(grad_wide)], 1), tables)
    back_wide = signal_of(conj_times(spectrum_kernel, spectrum_grad), tables)[:, :length]
    lagged = signal_of(conj_times(input_spectrum, spectrum_grad), tables)
    chan_back, lagged = ((back_wide + own_skip * grad_wide).astype(jnp.bfloat16), lagged)
    input_grad = lax.all_to_all(chan_back, "seq", split_axis=1, concat_axis=0, tiled=True).T
    mix_wide = long_mix.astype(jnp.float32)
    mixed_out = (query_wide * mix_wide).astype(jnp.bfloat16)
    reversed_part = jnp.concatenate([lagged[:, :1], lagged[:, length + 1 :][:, ::-1]], 1)
    filter_grad = (lagged[:, :length] + mirror_rows(reversed_part)) * factor_root
    input_back = input_grad.astype(jnp.float32)
    gated = jnp.stack(
        [out_grad.astype(jnp.float32) * mix_wide, input_back * value_wide, input_back * key_wide]
    )
    following = passed_along(gated[:, :2], "seq", -1)
    widened = jnp.concatenate([gated, following], 1)
    tap_grads = (
        tap_rows[:, 0] * widened[:, 0:positions]
        + tap_rows[:, 1] * widened[:, 1 : positions + 1]
        + tap_rows[:, 2] * widened[:, 2 : positions + 2]
    )
    tap_grads = tap_grads.astype(jnp.bfloat16)
    return (mixed_out, tap_grads[0], tap_grads[1], tap_grads[2], filter_grad)


def solution(mesh):
    in_specs = (
        P("seq", "chan"),
        P("seq", "chan"),
        P("seq", "chan"),
        P(None, None, "chan"),
        P("chan"),
        P(("chan", "seq"), None),
        P("seq", "chan"),
    )
    out_specs = (
        P("seq", "chan"),
        P("seq", "chan"),
        P("seq", "chan"),
        P("seq", "chan"),
        P(("chan", "seq"), None),
    )
    n_seq, n_chan = mesh.shape["seq"], mesh.shape["chan"]

    def on_device(query_proj, key_proj, value_proj, short_taps, skip_gain, long_filter, out_grad):
        arguments = (
            query_proj, key_proj, value_proj, short_taps, skip_gain, long_filter, out_grad
        )
        rows, width = query_proj.shape
        channels, length = long_filter.shape
        if (
            rows == channels == BLOCK
            and n_seq % 2 == 0
            and n_chan % 2 == 0
            and length <= 1024
        ):
            tables = transform_tables(length)
            return dense_device(n_seq, n_chan, tables, *arguments)
        return per_device(*arguments)

    return jax.shard_map(
        on_device, mesh=mesh, in_specs=in_specs, out_specs=out_specs, check_vma=False
    )
```

```python
import functools
import math

import jax
import jax.numpy as jnp
import ml_dtypes
import numpy as np
from jax import lax
from jax.experimental import pallas as pl
from jax.experimental.pallas import tpu as pltpu
from jax.sharding import PartitionSpec as P

F32 = jnp.float32
BF16 = jnp.bfloat16
BLOCK = 128


def transform_tables(length):
    odd = 2 * np.arange(length, dtype=np.int64) + 1
    counts = odd[:, None] * np.arange(length, dtype=np.int64)[None, :] % (4 * length)
    angles = counts * (math.pi / (2 * length))
    forward = np.concatenate([np.cos(angles), np.sin(angles)], 0)
    forward = forward.astype(ml_dtypes.bfloat16)
    return forward, np.ascontiguousarray(forward.T)


def dense_kernel(
    n_seq,
    n_chan,
    query_hbm,
    key_hbm,
    value_hbm,
    taps_ref,
    skip_ref,
    filter_hbm,
    cotangent_hbm,
    forward_hbm,
    inverse_hbm,
    mixed_hbm,
    query_grad_hbm,
    key_grad_hbm,
    value_grad_hbm,
    filter_grad_hbm,
    arguments,
    filter_ref,
    outputs,
    filter_grad_ref,
    forward,
    inverse,
    extended,
    shorted,
    gated,
    halo_out,
    halo_in,
    block_out,
    block_in,
    result_out,
    result_in,
    filter_out,
    filter_in,
    skip_in,
    terms_out,
    terms_in,
    spectra,
    products,
    even_part,
    odd_part,
    lag_spectra,
    kernel_spectra,
    halo_sent,
    halo_got,
    block_sent,
    block_got,
    result_sent,
    result_got,
    single_sent,
    single_got,
    table_got,
    argument_got,
    output_sent,
):
    rows = query_hbm.shape[0]
    length = filter_hbm.shape[1]
    chunk = 2 * rows
    chunks = length // chunk
    me = lax.axis_index("seq")
    chan = lax.axis_index("chan")
    is_owner = chan % 2 == 0
    not_owner = chan % 2 == 1
    owner_chan = jnp.where(is_owner, chan, n_chan - 1 - chan)
    other_chan = n_chan - 1 - owner_chan
    side = chan % 2
    mirrored_seq = n_seq - 1 - me

    def device(seq, chan_index):
        return {"seq": seq, "chan": chan_index}

    def remote(source, target, sent, got, where):
        return pltpu.make_async_remote_copy(
            src_ref=source,
            dst_ref=target,
            send_sem=sent,
            recv_sem=got,
            device_id=where,
            device_id_type=pl.DeviceIdType.MESH,
        )

    def await_on(buffer, semaphore):
        pltpu.make_async_copy(buffer, buffer, semaphore).wait()

    def lanes_of(block):
        return pl.ds(pl.multiple_of(block * BLOCK, BLOCK), BLOCK)

    forward_copy = pltpu.make_async_copy(forward_hbm, forward, table_got.at[0])
    inverse_copy = pltpu.make_async_copy(inverse_hbm, inverse, table_got.at[1])

    argument_copies = [
        pltpu.make_async_copy(source, arguments.at[p], argument_got.at[p])
        for p, source in enumerate((query_hbm, key_hbm, value_hbm, cotangent_hbm))
    ]
    filter_load = pltpu.make_async_copy(filter_hbm, filter_ref, argument_got.at[4])
    for copy in argument_copies:
        copy.start()
    filter_load.start()

    barrier = pltpu.get_barrier_semaphore()

    def greet(index, carry):
        seq = index % n_seq
        target = jnp.where(index < n_seq, owner_chan, other_chan)

        @pl.when(jnp.logical_or(seq != me, target != chan))
        def _():
            pl.semaphore_signal(
                barrier,
                inc=1,
                device_id=device(seq, target),
                device_id_type=pl.DeviceIdType.MESH,
            )

        return carry

    lax.fori_loop(0, 2 * n_seq, greet, 0)

    @pl.when(is_owner)
    def _():
        forward_copy.start()
        inverse_copy.start()

    for p in range(4):
        argument_copies[p].wait()
        extended[p, 8 : rows + 8, :] = arguments[p].astype(F32)
    halo_out[0] = jnp.concatenate([extended[p, rows + 6 : rows + 8, :] for p in range(4)], 0)
    halo_out[1] = jnp.concatenate([extended[p, 8:10, :] for p in range(4)], 0)

    pl.semaphore_wait(barrier, 2 * n_seq - 1)

    to_next = remote(
        halo_out.at[0],
        halo_in.at[0],
        halo_sent.at[0],
        halo_got.at[0],
        device(jnp.minimum(me + 1, n_seq - 1), chan),
    )
    to_previous = remote(
        halo_out.at[1],
        halo_in.at[1],
        halo_sent.at[1],
        halo_got.at[1],
        device(jnp.maximum(me - 1, 0), chan),
    )

    @pl.when(me < n_seq - 1)
    def _():
        to_next.start()

    @pl.when(me > 0)
    def _():
        to_previous.start()

    filter_copy = remote(
        filter_out,
        filter_in,
        single_sent.at[0],
        single_got.at[0],
        device(mirrored_seq, owner_chan),
    )
    skip_copy = remote(
        skip_ref, skip_in, single_sent.at[1], single_got.at[1], device(mirrored_seq, owner_chan)
    )
    terms_copy = remote(
        terms_out, terms_in, single_sent.at[2], single_got.at[2], device(mirrored_seq, other_chan)
    )

    @pl.when(not_owner)
    def _():
        skip_copy.start()
        filter_load.wait()
        filter_out[...] = filter_ref[...].astype(BF16)
        filter_copy.start()

    @pl.when(me > 0)
    def _():
        await_on(halo_in.at[0], halo_got.at[0])

    @pl.when(me == 0)
    def _():
        halo_in[0] = jnp.zeros(halo_in.shape[1:], F32)

    @pl.when(me < n_seq - 1)
    def _():
        await_on(halo_in.at[1], halo_got.at[1])

    @pl.when(me == n_seq - 1)
    def _():
        halo_in[1] = jnp.zeros(halo_in.shape[1:], F32)

    for p in range(4):
        extended[p, 6:8, :] = halo_in[0, 2 * p : 2 * p + 2, :]
        extended[p, rows + 8 : rows + 16, :] = jnp.concatenate(
            [halo_in[1, 2 * p : 2 * p + 2, :], jnp.zeros((6, halo_in.shape[2]), F32)], 0
        )

    def owner_of(block):
        return jnp.where(is_owner, block, n_seq - 1 - block)

    def send_block(step, carry):
        block = (me + n_seq // 2 + step) % n_seq
        lanes = lanes_of(block)
        for p in range(3):
            total = taps_ref[p, 0:1, lanes] * extended[p, 8 : rows + 16, lanes]
            total += taps_ref[p, 1:2, lanes] * extended[p, 7 : rows + 15, lanes]
            total += taps_ref[p, 2:3, lanes] * extended[p, 6 : rows + 14, lanes]
            shorted[p, :, lanes] = total.astype(BF16).astype(F32)
        product = shorted[1, 0:rows, lanes] * shorted[2, 0:rows, lanes]
        block_out[block, 0:rows, :] = product.astype(BF16)
        gate = extended[3, 8 : rows + 8, lanes] * shorted[0, 0:rows, lanes]
        block_out[block, rows : 2 * rows, :] = gate.astype(BF16)
        target = owner_of(block)
        here = jnp.logical_and(is_owner, block == me)

        @pl.when(here)
        def _():
            pltpu.make_async_copy(
                block_out.at[block], block_in.at[0, me], block_got.at[0, me]
            ).start()

        @pl.when(jnp.logical_not(here))
        def _():
            remote(
                block_out.at[block],
                block_in.at[side, me],
                block_sent.at[block],
                block_got.at[side, me],
                device(target, owner_chan),
            ).start()

        return carry

    lax.fori_loop(0, n_seq, send_block, 0)

    def columns_of(seq):
        return jnp.concatenate(
            [
                block_in[0, seq, 0:rows, :],
                block_in[1, seq, 0:rows, :],
                block_in[0, seq, rows : 2 * rows, :],
                block_in[1, seq, rows : 2 * rows, :],
            ],
            1,
        )

    wide = 2 * BLOCK

    @pl.when(is_owner)
    def _():
        scale = 1.0 / (length * math.sqrt(length))
        down = lax.broadcasted_iota(jnp.int32, (BLOCK, BLOCK), 0)
        across = lax.broadcasted_iota(jnp.int32, (BLOCK, BLOCK), 1)
        flip = jnp.where(down + across == BLOCK - 1, 1.0, 0.0).astype(BF16)

        def flipped(values):
            return jnp.dot(flip, values, preferred_element_type=F32)

        def halves(index):
            start = pl.multiple_of(index * chunk, chunk)
            return pl.ds(start, chunk), pl.ds(length + start, chunk)

        forward_copy.wait()
        filter_load.wait()
        await_on(filter_in, single_got.at[0])
        own = filter_ref[...]
        other = filter_in[...]
        own_flipped = flipped(own.astype(BF16))
        other_flipped = flipped(other)
        other = other.astype(F32)
        even_part[0:BLOCK, :] = (own + other_flipped).astype(BF16)
        even_part[BLOCK:, :] = (other + own_flipped).astype(BF16)
        odd_part[0:BLOCK, :] = (own - other_flipped).astype(BF16)
        odd_part[BLOCK:, :] = (other - own_flipped).astype(BF16)

        def kernel_transform(index, carry):
            first, second = halves(index)
            contracted = (((1,), (1,)), ((), ()))
            kernel_spectra[first, :] = lax.dot_general(
                forward[first, :], even_part[...], contracted, preferred_element_type=F32
            )
            kernel_spectra[second, :] = lax.dot_general(
                forward[second, :], odd_part[...], contracted, preferred_element_type=F32
            )
            return carry

        lax.fori_loop(0, chunks, kernel_transform, 0)

        for step in range(chunks):
            piece = (me // 2 + step) % chunks
            for half in range(2):
                for from_side in range(2):
                    seq = 2 * piece + half
                    await_on(block_in.at[from_side, seq], block_got.at[from_side, seq])
            columns = jnp.concatenate([columns_of(2 * piece), columns_of(2 * piece + 1)], 0)
            lags = pl.ds(pl.multiple_of(piece * chunk, chunk), chunk)

            def transform(index, carry):
                at = pl.ds(pl.multiple_of(index * chunk, chunk), chunk)
                term = jnp.dot(forward[at, lags], columns, preferred_element_type=F32)
                if step == 0:
                    spectra[at, :] = term
                else:
                    spectra[at, :] += term
                return carry

            lax.fori_loop(0, 2 * chunks, transform, 0)

        def spectral_products(index, carry):
            first, second = halves(index)
            kernel_cos, kernel_sin = kernel_spectra[first, :], kernel_spectra[second, :]
            input_cos, input_sin = spectra[first, 0:wide], spectra[second, 0:wide]
            grad_cos, grad_sin = spectra[first, wide:], spectra[second, wide:]
            mix_cos = kernel_cos * input_cos - kernel_sin * input_sin
            mix_sin = kernel_cos * input_sin + kernel_sin * input_cos
            back_cos = kernel_cos * grad_cos + kernel_sin * grad_sin
            back_sin = kernel_cos * grad_sin - kernel_sin * grad_cos
            products[first, 0:wide] = mix_cos.astype(BF16)
            products[second, 0:wide] = mix_sin.astype(BF16)
            products[first, wide:] = back_cos.astype(BF16)
            products[second, wide:] = back_sin.astype(BF16)
            return carry

        lax.fori_loop(0, chunks, spectral_products, 0)
        await_on(skip_in, single_got.at[1])
        gains = [skip_ref[pl.ds(me, 1), :], skip_in[pl.ds(mirrored_seq, 1), :]]
        gains = jnp.concatenate(gains + gains, 1)
        inverse_copy.wait()

        def send_result(seq):
            remote(
                result_out.at[1, seq],
                result_in.at[mirrored_seq],
                result_sent.at[1, seq],
                result_got.at[mirrored_seq],
                device(seq, other_chan),
            ).start()

            @pl.when(seq == me)
            def _():
                pltpu.make_async_copy(
                    result_out.at[0, me], result_in.at[me], result_got.at[me]
                ).start()

            @pl.when(seq != me)
            def _():
                remote(
                    result_out.at[0, seq],
                    result_in.at[me],
                    result_sent.at[0, seq],
                    result_got.at[me],
                    device(seq, owner_chan),
                ).start()

        first_piece = (me // 2 + chunks // 2) % chunks
        for to_side in range(2):
            result_out[to_side, n_seq - 1, 2 * rows :, :] = jnp.zeros((16, BLOCK), BF16)

        def results(step, carry):
            index = (first_piece + chunks - step) % chunks
            at = pl.ds(pl.multiple_of(index * chunk, chunk), chunk)
            sums = jnp.dot(inverse[at, :], products[...], preferred_element_type=F32) * scale
            for half in range(2):
                seq = 2 * index + half
                here = sums[half * rows : (half + 1) * rows]
                here = here + gains * columns_of(seq).astype(F32)
                before = (seq + n_seq - 1) % n_seq
                for to_side in range(2):
                    mix = here[:, to_side * BLOCK : (to_side + 1) * BLOCK]
                    back = here[:, wide + to_side * BLOCK : wide + (to_side + 1) * BLOCK]
                    result_out[to_side, seq, 0:rows, :] = mix.astype(BF16)
                    result_out[to_side, seq, rows : 2 * rows, :] = back.astype(BF16)
                    edge = jnp.concatenate([mix[0:2], back[0:2], jnp.zeros((12, BLOCK), F32)], 0)

                    @pl.when(seq > 0)
                    def _():
                        result_out[to_side, before, 2 * rows :, :] = edge.astype(BF16)

            @pl.when(step > 0)
            def _():
                send_result(2 * index + 1)

            send_result(2 * index)
            return carry

        lax.fori_loop(0, chunks, results, 0)
        send_result(2 * first_piece + 1)

        def lag_products(index, carry):
            first, second = halves(index)
            input_cos, input_sin = spectra[first, 0:wide], spectra[second, 0:wide]
            grad_cos, grad_sin = spectra[first, wide:], spectra[second, wide:]
            real = input_cos * grad_cos + input_sin * grad_sin
            imag = input_sin * grad_cos - input_cos * grad_sin
            lag_spectra[:, first] = real.T.astype(BF16)
            lag_spectra[:, second] = imag.T.astype(BF16)
            return carry

        lax.fori_loop(0, chunks, lag_products, 0)
        def filter_terms(index, carry):
            lags = pl.ds(pl.multiple_of(index * chunk, chunk), chunk)
            cosine = jnp.dot(
                lag_spectra[:, 0:length], forward[0:length, lags], preferred_element_type=F32
            )
            sine = jnp.dot(
                lag_spectra[:, length:], forward[length:, lags], preferred_element_type=F32
            )
            ahead = cosine - sine
            behind = (cosine + sine).astype(BF16)
            terms_out[:, lags] = ((ahead[BLOCK:] + flipped(behind[:BLOCK])) * scale).astype(BF16)
            filter_grad_ref[:, lags] = (ahead[:BLOCK] + flipped(behind[BLOCK:])) * scale
            return carry

        lax.fori_loop(0, chunks, filter_terms, 0)
        terms_copy.start()

    targets = (mixed_hbm, query_grad_hbm, key_grad_hbm, value_grad_hbm)
    filter_store = pltpu.make_async_copy(filter_grad_ref, filter_grad_hbm, output_sent.at[4])

    @pl.when(is_owner)
    def _():
        filter_store.start()

    def finish_block(step, carry):
        source = (me + n_seq // 2 + step) % n_seq
        block = owner_of(source)
        lanes = lanes_of(block)
        await_on(result_in.at[block], result_got.at[block])
        edge = result_in[block, 2 * rows :, :].astype(F32)
        mix = result_in[block, 0:rows, :].astype(F32)
        back = result_in[block, rows : 2 * rows, :].astype(F32)
        spare = jnp.zeros((6, BLOCK), F32)
        outputs[0, :, lanes] = (shorted[0, 0:rows, lanes] * mix).astype(BF16)
        mix = jnp.concatenate([mix, edge[0:2], spare], 0)
        back = jnp.concatenate([back, edge[2:4], spare], 0)
        gated[0] = extended[3, 8 : rows + 16, lanes] * mix
        gated[1] = back * shorted[2, :, lanes]
        gated[2] = back * shorted[1, :, lanes]
        for p in range(3):
            total = taps_ref[p, 0:1, lanes] * gated[p, 0:rows, :]
            total += taps_ref[p, 1:2, lanes] * gated[p, 1 : rows + 1, :]
            total += taps_ref[p, 2:3, lanes] * gated[p, 2 : rows + 2, :]
            outputs[p + 1, :, lanes] = total.astype(BF16)
        for p, target in enumerate(targets):
            pltpu.make_async_copy(
                outputs.at[p, :, lanes], target.at[:, lanes], output_sent.at[p]
            ).start()
        return carry

    lax.fori_loop(0, n_seq, finish_block, 0)

    @pl.when(not_owner)
    def _():
        await_on(terms_in, single_got.at[2])
        filter_grad_ref[...] = terms_in[...].astype(F32)
        filter_store.start()
        filter_copy.wait_send()
        skip_copy.wait_send()

    @pl.when(me < n_seq - 1)
    def _():
        to_next.wait_send()

    @pl.when(me > 0)
    def _():
        to_previous.wait_send()

    for p, target in enumerate(targets):
        pltpu.make_async_copy(outputs.at[p], target, output_sent.at[p]).wait()
    filter_store.wait()

    def drain_block(block, carry):
        @pl.when(jnp.logical_or(not_owner, block != me))
        def _():
            await_on(block_out.at[block], block_sent.at[block])

        return carry

    lax.fori_loop(0, n_seq, drain_block, 0)

    @pl.when(is_owner)
    def _():
        terms_copy.wait_send()

        def drain_result(seq, carry):
            await_on(result_out.at[1, seq], result_sent.at[1, seq])

            @pl.when(seq != me)
            def _():
                await_on(result_out.at[0, seq], result_sent.at[0, seq])

            return carry

        lax.fori_loop(0, n_seq, drain_result, 0)


def hand_over(*refs):
    sources, targets, done = refs[:5], refs[5:10], refs[10]
    copies = [
        pltpu.make_async_copy(source, target, done.at[index])
        for index, (source, target) in enumerate(zip(sources, targets))
    ]
    for copy in copies:
        copy.start()
    for copy in copies:
        copy.wait()


def dense_device(
    n_seq, n_chan, tables, query, key, value, short_taps, skip_gain, long_filter, cotangent
):
    rows, width = query.shape
    channels, length = long_filter.shape
    whole = pl.BlockSpec(memory_space=pltpu.VMEM)
    apart = pl.BlockSpec(memory_space=pl.ANY)
    sequence_like = jax.ShapeDtypeStruct((rows, width), BF16)
    wide = 2 * channels
    semaphores = pltpu.SemaphoreType.DMA
    results = pl.pallas_call(
        functools.partial(dense_kernel, n_seq, n_chan),
        out_shape=(sequence_like,) * 4 + (jax.ShapeDtypeStruct((channels, length), F32),),
        in_specs=[apart] * 3 + [whole] * 2 + [apart] * 4,
        out_specs=(apart,) * 5,
        scratch_shapes=[
            pltpu.VMEM((4, rows, width), BF16),
            pltpu.VMEM((channels, length), F32),
            pltpu.VMEM((4, rows, width), BF16),
            pltpu.VMEM((channels, length), F32),
            pltpu.VMEM((2 * length, length), BF16),
            pltpu.VMEM((length, 2 * length), BF16),
            pltpu.VMEM((4, rows + 16, width), F32),
            pltpu.VMEM((3, rows + 8, width), F32),
            pltpu.VMEM((3, rows + 8, channels), F32),
            pltpu.VMEM((2, 8, width), F32),
            pltpu.VMEM((2, 8, width), F32),
            pltpu.VMEM((n_seq, 2 * rows, channels), BF16),
            pltpu.VMEM((2, n_seq, 2 * rows, channels), BF16),
            pltpu.VMEM((2, n_seq, 2 * rows + 16, channels), BF16),
            pltpu.VMEM((n_seq, 2 * rows + 16, channels), BF16),
            pltpu.VMEM((channels, length), BF16),
            pltpu.VMEM((channels, length), BF16),
            pltpu.VMEM((n_seq, channels), F32),
            pltpu.VMEM((channels, length), BF16),
            pltpu.VMEM((channels, length), BF16),
            pltpu.VMEM((2 * length, 2 * wide), F32),
            pltpu.VMEM((2 * length, 2 * wide), BF16),
            pltpu.VMEM((wide, length), BF16),
            pltpu.VMEM((wide, length), BF16),
            pltpu.VMEM((wide, 2 * length), BF16),
            pltpu.VMEM((2 * length, wide), F32),
            semaphores((2,)),
            semaphores((2,)),
            semaphores((n_seq,)),
            semaphores((2, n_seq)),
            semaphores((2, n_seq)),
            semaphores((n_seq,)),
            semaphores((3,)),
            semaphores((3,)),
            semaphores((2,)),
            semaphores((5,)),
            semaphores((5,)),
        ],
        compiler_params=pltpu.CompilerParams(
            collective_id=0, has_side_effects=True, vmem_limit_bytes=56 * 1024 * 1024
        ),
    )(
        query,
        key,
        value,
        short_taps,
        skip_gain.reshape(n_seq, channels),
        long_filter,
        cotangent,
        *[jnp.asarray(table) for table in tables],
    )
    return pl.pallas_call(
        hand_over,
        out_shape=[jax.ShapeDtypeStruct(result.shape, result.dtype) for result in results],
        in_specs=[apart] * 5,
        out_specs=[apart] * 5,
        scratch_shapes=[semaphores((5,))],
        compiler_params=pltpu.CompilerParams(vmem_limit_bytes=56 * 1024 * 1024),
    )(*results)


exact_mode = lax.Precision.HIGHEST


def from_partner(array, axis, stride):
    return lax.ppermute(array, axis, [(i, i ^ 1 << stride) for i in range(lax.axis_size(axis))])


def passed_along(array, axis, by):
    length = lax.axis_size(axis)
    pairs = [(i, i + by) for i in range(length) if 0 <= i + by < length]
    return lax.ppermute(array, axis, pairs)


def divisor_pair(total_size):
    first_side = 1
    for candidate in range(1, math.isqrt(total_size) + 1):
        if total_size % candidate == 0:
            first_side = candidate
    return (first_side, total_size // first_side)


def angle_table(height, across, period):
    counts = (
        jnp.arange(height, dtype=jnp.int32)[:, None]
        * jnp.arange(across, dtype=jnp.int32)[None, :]
        % period
    )
    angles = counts.astype(jnp.float32) * (2.0 * math.pi / period)
    return (jnp.cos(angles), jnp.sin(angles))


def make_tables(total_size):
    first_side, second_side = divisor_pair(total_size)
    return (
        angle_table(first_side, first_side, first_side),
        angle_table(first_side, second_side, total_size),
        angle_table(second_side, second_side, second_side),
        first_side,
        second_side,
    )


def right_product(values, matrix):
    return jnp.einsum("ckm,ml->ckl", values, matrix, precision=exact_mode)


def left_product(matrix, values):
    return jnp.einsum("kn,cnm->ckm", matrix, values, precision=exact_mode)


def spectrum_of(signal, tables):
    (
        (cos_first, sin_first),
        (cosine_rotation, sin_twist),
        (cos_second, sin_second),
        first_side,
        second_side,
    ) = tables
    shaped = signal.reshape(signal.shape[0], first_side, second_side)
    section_real = left_product(cos_first, shaped)
    section_imag = -left_product(sin_first, shaped)
    twist_real = section_real * cosine_rotation + section_imag * sin_twist
    twist_imag = section_imag * cosine_rotation - section_real * sin_twist
    return (
        right_product(twist_real, cos_second) + right_product(twist_imag, sin_second),
        right_product(twist_imag, cos_second) - right_product(twist_real, sin_second),
    )


def signal_of(spectrum, tables):
    (
        (cos_first, sin_first),
        (cosine_rotation, sin_twist),
        (cos_second, sin_second),
        first_side,
        second_side,
    ) = tables
    spec_real, spec_imag = spectrum
    section_real = right_product(spec_real, cos_second) - right_product(spec_imag, sin_second)
    section_imag = right_product(spec_imag, cos_second) + right_product(spec_real, sin_second)
    twist_real = section_real * cosine_rotation - section_imag * sin_twist
    twist_imag = section_imag * cosine_rotation + section_real * sin_twist
    result = left_product(cos_first, twist_real) - left_product(sin_first, twist_imag)
    return result.reshape(result.shape[0], -1) / (first_side * second_side)


def times_spec(former, latter):
    return (
        former[0] * latter[0] - former[1] * latter[1],
        former[0] * latter[1] + former[1] * latter[0],
    )


def conj_times(former, latter):
    return (
        former[0] * latter[0] + former[1] * latter[1],
        former[0] * latter[1] - former[1] * latter[0],
    )


def mirror_rows(block_rows):
    mirrored = block_rows
    for bit_index in range((lax.axis_size("seq") * lax.axis_size("chan")).bit_length() - 1):
        mirrored = from_partner(mirrored, ("seq", "chan"), bit_index)
    return mirrored[::-1]


def per_device(query_proj, key_proj, value_proj, short_taps, skip_gain, long_filter, out_grad):
    positions = query_proj.shape[0]
    channels, length = long_filter.shape
    doubled = 2 * length
    factor_root = 1.0 / math.sqrt(length)
    tables = make_tables(doubled)
    own_skip = lax.dynamic_slice_in_dim(skip_gain, lax.axis_index("seq") * channels, channels)[
        :, None
    ]
    stacked = jnp.stack([query_proj, key_proj, value_proj])
    previous = passed_along(stacked[:, positions - 2 :], "seq", 1)
    extended = jnp.concatenate([previous, stacked], 1).astype(jnp.float32)
    tap_rows = short_taps[:, :, None, :]
    shorted = (
        tap_rows[:, 0] * extended[:, 2 : positions + 2]
        + tap_rows[:, 1] * extended[:, 1 : positions + 1]
        + tap_rows[:, 2] * extended[:, 0:positions]
    )
    shorted = shorted.astype(jnp.bfloat16)
    query_short, key_short, value_short = (shorted[0], shorted[1], shorted[2])
    key_wide = key_short.astype(jnp.float32)
    value_wide = value_short.astype(jnp.float32)
    product_in = (key_wide * value_wide).astype(jnp.bfloat16)
    kernel_own = long_filter * factor_root
    kernel_mirror = mirror_rows(kernel_own)
    zero_column = jnp.zeros((channels, 1), jnp.float32)
    kernel_full = jnp.concatenate(
        [
            kernel_own[:, :1] + kernel_mirror[:, :1],
            kernel_own[:, 1:],
            zero_column,
            kernel_mirror[:, 1:][:, ::-1],
        ],
        1,
    )
    spectrum_kernel = spectrum_of(kernel_full, tables)
    query_wide = query_short.astype(jnp.float32)
    chan_product = lax.all_to_all(product_in.T, "seq", split_axis=0, concat_axis=1, tiled=True)
    input_wide = chan_product.astype(jnp.float32)
    input_spectrum = spectrum_of(
        jnp.concatenate([input_wide, jnp.zeros_like(input_wide)], 1), tables
    )
    mixed_wide = signal_of(times_spec(spectrum_kernel, input_spectrum), tables)[:, :length]
    chan_mix, input_spectrum = (
        (mixed_wide + own_skip * input_wide).astype(jnp.bfloat16),
        input_spectrum,
    )
    long_mix = lax.all_to_all(chan_mix, "seq", split_axis=1, concat_axis=0, tiled=True).T
    gate_grad = (out_grad.astype(jnp.float32) * query_wide).astype(jnp.bfloat16)
    chan_gate = lax.all_to_all(gate_grad.T, "seq", split_axis=0, concat_axis=1, tiled=True)
    grad_wide = chan_gate.astype(jnp.float32)
    spectrum_grad = spectrum_of(jnp.concatenate([grad_wide, jnp.zeros_like(grad_wide)], 1), tables)
    back_wide = signal_of(conj_times(spectrum_kernel, spectrum_grad), tables)[:, :length]
    lagged = signal_of(conj_times(input_spectrum, spectrum_grad), tables)
    chan_back, lagged = ((back_wide + own_skip * grad_wide).astype(jnp.bfloat16), lagged)
    input_grad = lax.all_to_all(chan_back, "seq", split_axis=1, concat_axis=0, tiled=True).T
    mix_wide = long_mix.astype(jnp.float32)
    mixed_out = (query_wide * mix_wide).astype(jnp.bfloat16)
    reversed_part = jnp.concatenate([lagged[:, :1], lagged[:, length + 1 :][:, ::-1]], 1)
    filter_grad = (lagged[:, :length] + mirror_rows(reversed_part)) * factor_root
    input_back = input_grad.astype(jnp.float32)
    gated = jnp.stack(
        [out_grad.astype(jnp.float32) * mix_wide, input_back * value_wide, input_back * key_wide]
    )
    following = passed_along(gated[:, :2], "seq", -1)
    widened = jnp.concatenate([gated, following], 1)
    tap_grads = (
        tap_rows[:, 0] * widened[:, 0:positions]
        + tap_rows[:, 1] * widened[:, 1 : positions + 1]
        + tap_rows[:, 2] * widened[:, 2 : positions + 2]
    )
    tap_grads = tap_grads.astype(jnp.bfloat16)
    return (mixed_out, tap_grads[0], tap_grads[1], tap_grads[2], filter_grad)


def solution(mesh):
    in_specs = (
        P("seq", "chan"),
        P("seq", "chan"),
        P("seq", "chan"),
        P(None, None, "chan"),
        P("chan"),
        P(("chan", "seq"), None),
        P("seq", "chan"),
    )
    out_specs = (
        P("seq", "chan"),
        P("seq", "chan"),
        P("seq", "chan"),
        P("seq", "chan"),
        P(("chan", "seq"), None),
    )
    n_seq, n_chan = mesh.shape["seq"], mesh.shape["chan"]

    def on_device(query_proj, key_proj, value_proj, short_taps, skip_gain, long_filter, out_grad):
        arguments = (
            query_proj, key_proj, value_proj, short_taps, skip_gain, long_filter, out_grad
        )
        rows, width = query_proj.shape
        channels, length = long_filter.shape
        if (
            rows == channels == BLOCK
            and n_seq % 2 == 0
            and n_chan % 2 == 0
            and length <= 1024
        ):
            tables = transform_tables(length)
            return tuple(dense_device(n_seq, n_chan, tables, *arguments))
        return per_device(*arguments)

    return jax.shard_map(
        on_device, mesh=mesh, in_specs=in_specs, out_specs=out_specs, check_vma=False
    )
```

```python
import functools
import math

import jax
import jax.numpy as jnp
import ml_dtypes
import numpy as np
from jax import lax
from jax.experimental import pallas as pl
from jax.experimental.pallas import tpu as pltpu
from jax.sharding import PartitionSpec as P

F32 = jnp.float32
BF16 = jnp.bfloat16
BLOCK = 128


def transform_tables(length):
    odd = 2 * np.arange(length, dtype=np.int64) + 1
    counts = odd[:, None] * np.arange(length, dtype=np.int64)[None, :] % (4 * length)
    angles = counts * (math.pi / (2 * length))
    forward = np.concatenate([np.cos(angles), np.sin(angles)], 0)
    forward = forward.astype(ml_dtypes.bfloat16)
    return forward, np.ascontiguousarray(forward.T)


def dense_kernel(
    n_seq,
    n_chan,
    query_hbm,
    key_hbm,
    value_hbm,
    taps_ref,
    skip_ref,
    filter_hbm,
    cotangent_hbm,
    forward_hbm,
    inverse_hbm,
    mixed_hbm,
    query_grad_hbm,
    key_grad_hbm,
    value_grad_hbm,
    filter_grad_hbm,
    arguments,
    filter_ref,
    outputs,
    filter_grad_ref,
    forward,
    inverse,
    extended,
    shorted,
    gated,
    halo_out,
    halo_in,
    block_out,
    block_in,
    result_out,
    result_in,
    filter_out,
    filter_in,
    skip_in,
    terms_out,
    terms_in,
    spectra,
    products,
    even_part,
    odd_part,
    lag_spectra,
    kernel_spectra,
    halo_sent,
    halo_got,
    block_sent,
    block_got,
    result_sent,
    result_got,
    single_sent,
    single_got,
    table_got,
    argument_got,
    output_sent,
):
    rows = query_hbm.shape[0]
    length = filter_hbm.shape[1]
    chunk = 2 * rows
    chunks = length // chunk
    me = lax.axis_index("seq")
    chan = lax.axis_index("chan")
    is_owner = chan % 2 == 0
    not_owner = chan % 2 == 1
    owner_chan = jnp.where(is_owner, chan, n_chan - 1 - chan)
    other_chan = n_chan - 1 - owner_chan
    side = chan % 2
    mirrored_seq = n_seq - 1 - me

    def device(seq, chan_index):
        return {"seq": seq, "chan": chan_index}

    def remote(source, target, sent, got, where):
        return pltpu.make_async_remote_copy(
            src_ref=source,
            dst_ref=target,
            send_sem=sent,
            recv_sem=got,
            device_id=where,
            device_id_type=pl.DeviceIdType.MESH,
        )

    def await_on(buffer, semaphore):
        pltpu.make_async_copy(buffer, buffer, semaphore).wait()

    def lanes_of(block):
        return pl.ds(pl.multiple_of(block * BLOCK, BLOCK), BLOCK)

    forward_copy = pltpu.make_async_copy(forward_hbm, forward, table_got.at[0])
    inverse_copy = pltpu.make_async_copy(inverse_hbm, inverse, table_got.at[1])

    argument_copies = [
        pltpu.make_async_copy(source, arguments.at[p], argument_got.at[p])
        for p, source in enumerate((query_hbm, key_hbm, value_hbm, cotangent_hbm))
    ]
    filter_load = pltpu.make_async_copy(filter_hbm, filter_ref, argument_got.at[4])
    for copy in argument_copies:
        copy.start()
    filter_load.start()

    barrier = pltpu.get_barrier_semaphore()

    def greet(index, carry):
        seq = index % n_seq
        target = jnp.where(index < n_seq, owner_chan, other_chan)

        @pl.when(jnp.logical_or(seq != me, target != chan))
        def _():
            pl.semaphore_signal(
                barrier,
                inc=1,
                device_id=device(seq, target),
                device_id_type=pl.DeviceIdType.MESH,
            )

        return carry

    lax.fori_loop(0, 2 * n_seq, greet, 0)

    @pl.when(is_owner)
    def _():
        forward_copy.start()
        inverse_copy.start()

    for p in range(4):
        argument_copies[p].wait()
        extended[p, 8 : rows + 8, :] = arguments[p].astype(F32)
    halo_out[0] = jnp.concatenate([extended[p, rows + 6 : rows + 8, :] for p in range(4)], 0)
    halo_out[1] = jnp.concatenate([extended[p, 8:10, :] for p in range(4)], 0)

    pl.semaphore_wait(barrier, 2 * n_seq - 1)

    to_next = remote(
        halo_out.at[0],
        halo_in.at[0],
        halo_sent.at[0],
        halo_got.at[0],
        device(jnp.minimum(me + 1, n_seq - 1), chan),
    )
    to_previous = remote(
        halo_out.at[1],
        halo_in.at[1],
        halo_sent.at[1],
        halo_got.at[1],
        device(jnp.maximum(me - 1, 0), chan),
    )

    @pl.when(me < n_seq - 1)
    def _():
        to_next.start()

    @pl.when(me > 0)
    def _():
        to_previous.start()

    filter_copy = remote(
        filter_out,
        filter_in,
        single_sent.at[0],
        single_got.at[0],
        device(mirrored_seq, owner_chan),
    )
    skip_copy = remote(
        skip_ref, skip_in, single_sent.at[1], single_got.at[1], device(mirrored_seq, owner_chan)
    )
    terms_copy = remote(
        terms_out, terms_in, single_sent.at[2], single_got.at[2], device(mirrored_seq, other_chan)
    )

    @pl.when(not_owner)
    def _():
        skip_copy.start()
        filter_load.wait()
        filter_out[...] = filter_ref[...].astype(BF16)
        filter_copy.start()

    @pl.when(me > 0)
    def _():
        await_on(halo_in.at[0], halo_got.at[0])

    @pl.when(me == 0)
    def _():
        halo_in[0] = jnp.zeros(halo_in.shape[1:], F32)

    @pl.when(me < n_seq - 1)
    def _():
        await_on(halo_in.at[1], halo_got.at[1])

    @pl.when(me == n_seq - 1)
    def _():
        halo_in[1] = jnp.zeros(halo_in.shape[1:], F32)

    for p in range(4):
        extended[p, 6:8, :] = halo_in[0, 2 * p : 2 * p + 2, :]
        extended[p, rows + 8 : rows + 16, :] = jnp.concatenate(
            [halo_in[1, 2 * p : 2 * p + 2, :], jnp.zeros((6, halo_in.shape[2]), F32)], 0
        )

    def owner_of(block):
        return jnp.where(is_owner, block, n_seq - 1 - block)

    def send_block(step, carry):
        block = (me + n_seq // 2 + step) % n_seq
        lanes = lanes_of(block)
        for p in range(3):
            total = taps_ref[p, 0:1, lanes] * extended[p, 8 : rows + 16, lanes]
            total += taps_ref[p, 1:2, lanes] * extended[p, 7 : rows + 15, lanes]
            total += taps_ref[p, 2:3, lanes] * extended[p, 6 : rows + 14, lanes]
            shorted[p, :, lanes] = total.astype(BF16).astype(F32)
        product = shorted[1, 0:rows, lanes] * shorted[2, 0:rows, lanes]
        block_out[block, 0:rows, :] = product.astype(BF16)
        gate = extended[3, 8 : rows + 8, lanes] * shorted[0, 0:rows, lanes]
        block_out[block, rows : 2 * rows, :] = gate.astype(BF16)
        target = owner_of(block)
        here = jnp.logical_and(is_owner, block == me)

        @pl.when(here)
        def _():
            pltpu.make_async_copy(
                block_out.at[block], block_in.at[0, me], block_got.at[0, me]
            ).start()

        @pl.when(jnp.logical_not(here))
        def _():
            remote(
                block_out.at[block],
                block_in.at[side, me],
                block_sent.at[block],
                block_got.at[side, me],
                device(target, owner_chan),
            ).start()

        return carry

    lax.fori_loop(0, n_seq, send_block, 0)

    def columns_of(seq):
        return jnp.concatenate(
            [
                block_in[0, seq, 0:rows, :],
                block_in[1, seq, 0:rows, :],
                block_in[0, seq, rows : 2 * rows, :],
                block_in[1, seq, rows : 2 * rows, :],
            ],
            1,
        )

    wide = 2 * BLOCK

    @pl.when(is_owner)
    def _():
        scale = 1.0 / (length * math.sqrt(length))
        down = lax.broadcasted_iota(jnp.int32, (BLOCK, BLOCK), 0)
        across = lax.broadcasted_iota(jnp.int32, (BLOCK, BLOCK), 1)
        flip = jnp.where(down + across == BLOCK - 1, 1.0, 0.0).astype(BF16)

        def flipped(values):
            return jnp.dot(flip, values, preferred_element_type=F32)

        def halves(index):
            start = pl.multiple_of(index * chunk, chunk)
            return pl.ds(start, chunk), pl.ds(length + start, chunk)

        forward_copy.wait()
        filter_load.wait()
        await_on(filter_in, single_got.at[0])
        own = filter_ref[...]
        other = filter_in[...]
        own_flipped = flipped(own.astype(BF16))
        other_flipped = flipped(other)
        other = other.astype(F32)
        even_part[0:BLOCK, :] = (own + other_flipped).astype(BF16)
        even_part[BLOCK:, :] = (other + own_flipped).astype(BF16)
        odd_part[0:BLOCK, :] = (own - other_flipped).astype(BF16)
        odd_part[BLOCK:, :] = (other - own_flipped).astype(BF16)

        def kernel_transform(index, carry):
            first, second = halves(index)
            contracted = (((1,), (1,)), ((), ()))
            kernel_spectra[first, :] = lax.dot_general(
                forward[first, :], even_part[...], contracted, preferred_element_type=F32
            )
            kernel_spectra[second, :] = lax.dot_general(
                forward[second, :], odd_part[...], contracted, preferred_element_type=F32
            )
            return carry

        lax.fori_loop(0, chunks, kernel_transform, 0)

        for step in range(chunks):
            piece = (me // 2 + step) % chunks
            for half in range(2):
                for from_side in range(2):
                    seq = 2 * piece + half
                    await_on(block_in.at[from_side, seq], block_got.at[from_side, seq])
            columns = jnp.concatenate([columns_of(2 * piece), columns_of(2 * piece + 1)], 0)
            lags = pl.ds(pl.multiple_of(piece * chunk, chunk), chunk)

            def transform(index, carry):
                at = pl.ds(pl.multiple_of(index * chunk, chunk), chunk)
                term = jnp.dot(forward[at, lags], columns, preferred_element_type=F32)
                if step == 0:
                    spectra[at, :] = term
                else:
                    spectra[at, :] += term
                return carry

            lax.fori_loop(0, 2 * chunks, transform, 0)

        def spectral_products(index, carry):
            first, second = halves(index)
            kernel_cos, kernel_sin = kernel_spectra[first, :], kernel_spectra[second, :]
            input_cos, input_sin = spectra[first, 0:wide], spectra[second, 0:wide]
            grad_cos, grad_sin = spectra[first, wide:], spectra[second, wide:]
            mix_cos = kernel_cos * input_cos - kernel_sin * input_sin
            mix_sin = kernel_cos * input_sin + kernel_sin * input_cos
            back_cos = kernel_cos * grad_cos + kernel_sin * grad_sin
            back_sin = kernel_cos * grad_sin - kernel_sin * grad_cos
            products[first, 0:wide] = mix_cos.astype(BF16)
            products[second, 0:wide] = mix_sin.astype(BF16)
            products[first, wide:] = back_cos.astype(BF16)
            products[second, wide:] = back_sin.astype(BF16)
            return carry

        lax.fori_loop(0, chunks, spectral_products, 0)
        await_on(skip_in, single_got.at[1])
        gains = [skip_ref[pl.ds(me, 1), :], skip_in[pl.ds(mirrored_seq, 1), :]]
        gains = jnp.concatenate(gains + gains, 1)
        inverse_copy.wait()

        def send_result(seq):
            remote(
                result_out.at[1, seq],
                result_in.at[mirrored_seq],
                result_sent.at[1, seq],
                result_got.at[mirrored_seq],
                device(seq, other_chan),
            ).start()

            @pl.when(seq == me)
            def _():
                pltpu.make_async_copy(
                    result_out.at[0, me], result_in.at[me], result_got.at[me]
                ).start()

            @pl.when(seq != me)
            def _():
                remote(
                    result_out.at[0, seq],
                    result_in.at[me],
                    result_sent.at[0, seq],
                    result_got.at[me],
                    device(seq, owner_chan),
                ).start()

        first_piece = (me // 2 + chunks // 2) % chunks
        for to_side in range(2):
            result_out[to_side, n_seq - 1, 2 * rows :, :] = jnp.zeros((16, BLOCK), BF16)

        def results(step, carry):
            index = (first_piece + chunks - step) % chunks
            at = pl.ds(pl.multiple_of(index * chunk, chunk), chunk)
            sums = jnp.dot(inverse[at, :], products[...], preferred_element_type=F32) * scale
            for half in range(2):
                seq = 2 * index + half
                here = sums[half * rows : (half + 1) * rows]
                here = here + gains * columns_of(seq).astype(F32)
                before = (seq + n_seq - 1) % n_seq
                for to_side in range(2):
                    mix = here[:, to_side * BLOCK : (to_side + 1) * BLOCK]
                    back = here[:, wide + to_side * BLOCK : wide + (to_side + 1) * BLOCK]
                    result_out[to_side, seq, 0:rows, :] = mix.astype(BF16)
                    result_out[to_side, seq, rows : 2 * rows, :] = back.astype(BF16)
                    edge = jnp.concatenate([mix[0:2], back[0:2], jnp.zeros((12, BLOCK), F32)], 0)

                    @pl.when(seq > 0)
                    def _():
                        result_out[to_side, before, 2 * rows :, :] = edge.astype(BF16)

            @pl.when(step > 0)
            def _():
                send_result(2 * index + 1)

            send_result(2 * index)
            return carry

        lax.fori_loop(0, chunks, results, 0)
        send_result(2 * first_piece + 1)

        def lag_products(index, carry):
            first, second = halves(index)
            input_cos, input_sin = spectra[first, 0:wide], spectra[second, 0:wide]
            grad_cos, grad_sin = spectra[first, wide:], spectra[second, wide:]
            real = input_cos * grad_cos + input_sin * grad_sin
            imag = input_sin * grad_cos - input_cos * grad_sin
            lag_spectra[:, first] = real.T.astype(BF16)
            lag_spectra[:, second] = imag.T.astype(BF16)
            return carry

        lax.fori_loop(0, chunks, lag_products, 0)
        def filter_terms(index, carry):
            lags = pl.ds(pl.multiple_of(index * chunk, chunk), chunk)
            cosine = jnp.dot(
                lag_spectra[:, 0:length], forward[0:length, lags], preferred_element_type=F32
            )
            sine = jnp.dot(
                lag_spectra[:, length:], forward[length:, lags], preferred_element_type=F32
            )
            ahead = cosine - sine
            behind = (cosine + sine).astype(BF16)
            terms_out[:, lags] = ((ahead[BLOCK:] + flipped(behind[:BLOCK])) * scale).astype(BF16)
            filter_grad_ref[:, lags] = (ahead[:BLOCK] + flipped(behind[BLOCK:])) * scale
            return carry

        lax.fori_loop(0, chunks, filter_terms, 0)
        terms_copy.start()

    targets = (mixed_hbm, query_grad_hbm, key_grad_hbm, value_grad_hbm)
    filter_store = pltpu.make_async_copy(filter_grad_ref, filter_grad_hbm, output_sent.at[4])

    @pl.when(is_owner)
    def _():
        filter_store.start()

    def finish_block(step, carry):
        source = (me + n_seq // 2 + step) % n_seq
        block = owner_of(source)
        lanes = lanes_of(block)
        await_on(result_in.at[block], result_got.at[block])
        edge = result_in[block, 2 * rows :, :].astype(F32)
        mix = result_in[block, 0:rows, :].astype(F32)
        back = result_in[block, rows : 2 * rows, :].astype(F32)
        spare = jnp.zeros((6, BLOCK), F32)
        outputs[0, :, lanes] = (shorted[0, 0:rows, lanes] * mix).astype(BF16)
        mix = jnp.concatenate([mix, edge[0:2], spare], 0)
        back = jnp.concatenate([back, edge[2:4], spare], 0)
        gated[0] = extended[3, 8 : rows + 16, lanes] * mix
        gated[1] = back * shorted[2, :, lanes]
        gated[2] = back * shorted[1, :, lanes]
        for p in range(3):
            total = taps_ref[p, 0:1, lanes] * gated[p, 0:rows, :]
            total += taps_ref[p, 1:2, lanes] * gated[p, 1 : rows + 1, :]
            total += taps_ref[p, 2:3, lanes] * gated[p, 2 : rows + 2, :]
            outputs[p + 1, :, lanes] = total.astype(BF16)
        for p, target in enumerate(targets):
            pltpu.make_async_copy(
                outputs.at[p, :, lanes], target.at[:, lanes], output_sent.at[p]
            ).start()
        return carry

    lax.fori_loop(0, n_seq, finish_block, 0)

    @pl.when(not_owner)
    def _():
        await_on(terms_in, single_got.at[2])
        filter_grad_ref[...] = terms_in[...].astype(F32)
        filter_store.start()
        filter_copy.wait_send()
        skip_copy.wait_send()

    @pl.when(me < n_seq - 1)
    def _():
        to_next.wait_send()

    @pl.when(me > 0)
    def _():
        to_previous.wait_send()

    for p, target in enumerate(targets):
        pltpu.make_async_copy(outputs.at[p], target, output_sent.at[p]).wait()
    filter_store.wait()

    def drain_block(block, carry):
        @pl.when(jnp.logical_or(not_owner, block != me))
        def _():
            await_on(block_out.at[block], block_sent.at[block])

        return carry

    lax.fori_loop(0, n_seq, drain_block, 0)

    @pl.when(is_owner)
    def _():
        terms_copy.wait_send()

        def drain_result(seq, carry):
            await_on(result_out.at[1, seq], result_sent.at[1, seq])

            @pl.when(seq != me)
            def _():
                await_on(result_out.at[0, seq], result_sent.at[0, seq])

            return carry

        lax.fori_loop(0, n_seq, drain_result, 0)


def hand_over(*refs):
    sources, targets, held = refs[:5], refs[5:10], refs[10:15]
    loaded, stored = refs[15], refs[16]
    loads = [
        pltpu.make_async_copy(sources[index], held[index], loaded.at[index]) for index in range(5)
    ]
    stores = [
        pltpu.make_async_copy(held[index], targets[index], stored.at[index]) for index in range(5)
    ]
    for load in loads:
        load.start()
    for load, store in zip(loads, stores):
        load.wait()
        store.start()
    for store in stores:
        store.wait()


def dense_device(
    n_seq, n_chan, tables, query, key, value, short_taps, skip_gain, long_filter, cotangent
):
    rows, width = query.shape
    channels, length = long_filter.shape
    whole = pl.BlockSpec(memory_space=pltpu.VMEM)
    apart = pl.BlockSpec(memory_space=pl.ANY)
    sequence_like = jax.ShapeDtypeStruct((rows, width), BF16)
    wide = 2 * channels
    semaphores = pltpu.SemaphoreType.DMA
    results = pl.pallas_call(
        functools.partial(dense_kernel, n_seq, n_chan),
        out_shape=(sequence_like,) * 4 + (jax.ShapeDtypeStruct((channels, length), F32),),
        in_specs=[apart] * 3 + [whole] * 2 + [apart] * 4,
        out_specs=(apart,) * 5,
        scratch_shapes=[
            pltpu.VMEM((4, rows, width), BF16),
            pltpu.VMEM((channels, length), F32),
            pltpu.VMEM((4, rows, width), BF16),
            pltpu.VMEM((channels, length), F32),
            pltpu.VMEM((2 * length, length), BF16),
            pltpu.VMEM((length, 2 * length), BF16),
            pltpu.VMEM((4, rows + 16, width), F32),
            pltpu.VMEM((3, rows + 8, width), F32),
            pltpu.VMEM((3, rows + 8, channels), F32),
            pltpu.VMEM((2, 8, width), F32),
            pltpu.VMEM((2, 8, width), F32),
            pltpu.VMEM((n_seq, 2 * rows, channels), BF16),
            pltpu.VMEM((2, n_seq, 2 * rows, channels), BF16),
            pltpu.VMEM((2, n_seq, 2 * rows + 16, channels), BF16),
            pltpu.VMEM((n_seq, 2 * rows + 16, channels), BF16),
            pltpu.VMEM((channels, length), BF16),
            pltpu.VMEM((channels, length), BF16),
            pltpu.VMEM((n_seq, channels), F32),
            pltpu.VMEM((channels, length), BF16),
            pltpu.VMEM((channels, length), BF16),
            pltpu.VMEM((2 * length, 2 * wide), F32),
            pltpu.VMEM((2 * length, 2 * wide), BF16),
            pltpu.VMEM((wide, length), BF16),
            pltpu.VMEM((wide, length), BF16),
            pltpu.VMEM((wide, 2 * length), BF16),
            pltpu.VMEM((2 * length, wide), F32),
            semaphores((2,)),
            semaphores((2,)),
            semaphores((n_seq,)),
            semaphores((2, n_seq)),
            semaphores((2, n_seq)),
            semaphores((n_seq,)),
            semaphores((3,)),
            semaphores((3,)),
            semaphores((2,)),
            semaphores((5,)),
            semaphores((5,)),
        ],
        compiler_params=pltpu.CompilerParams(
            collective_id=0, has_side_effects=True, vmem_limit_bytes=56 * 1024 * 1024
        ),
    )(
        query,
        key,
        value,
        short_taps,
        skip_gain.reshape(n_seq, channels),
        long_filter,
        cotangent,
        *[jnp.asarray(table) for table in tables],
    )
    return pl.pallas_call(
        hand_over,
        out_shape=[jax.ShapeDtypeStruct(result.shape, result.dtype) for result in results],
        in_specs=[apart] * 5,
        out_specs=[apart] * 5,
        scratch_shapes=[pltpu.VMEM(result.shape, result.dtype) for result in results]
        + [semaphores((5,)), semaphores((5,))],
        compiler_params=pltpu.CompilerParams(vmem_limit_bytes=56 * 1024 * 1024),
    )(*results)


exact_mode = lax.Precision.HIGHEST


def from_partner(array, axis, stride):
    return lax.ppermute(array, axis, [(i, i ^ 1 << stride) for i in range(lax.axis_size(axis))])


def passed_along(array, axis, by):
    length = lax.axis_size(axis)
    pairs = [(i, i + by) for i in range(length) if 0 <= i + by < length]
    return lax.ppermute(array, axis, pairs)


def divisor_pair(total_size):
    first_side = 1
    for candidate in range(1, math.isqrt(total_size) + 1):
        if total_size % candidate == 0:
            first_side = candidate
    return (first_side, total_size // first_side)


def angle_table(height, across, period):
    counts = (
        jnp.arange(height, dtype=jnp.int32)[:, None]
        * jnp.arange(across, dtype=jnp.int32)[None, :]
        % period
    )
    angles = counts.astype(jnp.float32) * (2.0 * math.pi / period)
    return (jnp.cos(angles), jnp.sin(angles))


def make_tables(total_size):
    first_side, second_side = divisor_pair(total_size)
    return (
        angle_table(first_side, first_side, first_side),
        angle_table(first_side, second_side, total_size),
        angle_table(second_side, second_side, second_side),
        first_side,
        second_side,
    )


def right_product(values, matrix):
    return jnp.einsum("ckm,ml->ckl", values, matrix, precision=exact_mode)


def left_product(matrix, values):
    return jnp.einsum("kn,cnm->ckm", matrix, values, precision=exact_mode)


def spectrum_of(signal, tables):
    (
        (cos_first, sin_first),
        (cosine_rotation, sin_twist),
        (cos_second, sin_second),
        first_side,
        second_side,
    ) = tables
    shaped = signal.reshape(signal.shape[0], first_side, second_side)
    section_real = left_product(cos_first, shaped)
    section_imag = -left_product(sin_first, shaped)
    twist_real = section_real * cosine_rotation + section_imag * sin_twist
    twist_imag = section_imag * cosine_rotation - section_real * sin_twist
    return (
        right_product(twist_real, cos_second) + right_product(twist_imag, sin_second),
        right_product(twist_imag, cos_second) - right_product(twist_real, sin_second),
    )


def signal_of(spectrum, tables):
    (
        (cos_first, sin_first),
        (cosine_rotation, sin_twist),
        (cos_second, sin_second),
        first_side,
        second_side,
    ) = tables
    spec_real, spec_imag = spectrum
    section_real = right_product(spec_real, cos_second) - right_product(spec_imag, sin_second)
    section_imag = right_product(spec_imag, cos_second) + right_product(spec_real, sin_second)
    twist_real = section_real * cosine_rotation - section_imag * sin_twist
    twist_imag = section_imag * cosine_rotation + section_real * sin_twist
    result = left_product(cos_first, twist_real) - left_product(sin_first, twist_imag)
    return result.reshape(result.shape[0], -1) / (first_side * second_side)


def times_spec(former, latter):
    return (
        former[0] * latter[0] - former[1] * latter[1],
        former[0] * latter[1] + former[1] * latter[0],
    )


def conj_times(former, latter):
    return (
        former[0] * latter[0] + former[1] * latter[1],
        former[0] * latter[1] - former[1] * latter[0],
    )


def mirror_rows(block_rows):
    mirrored = block_rows
    for bit_index in range((lax.axis_size("seq") * lax.axis_size("chan")).bit_length() - 1):
        mirrored = from_partner(mirrored, ("seq", "chan"), bit_index)
    return mirrored[::-1]


def per_device(query_proj, key_proj, value_proj, short_taps, skip_gain, long_filter, out_grad):
    positions = query_proj.shape[0]
    channels, length = long_filter.shape
    doubled = 2 * length
    factor_root = 1.0 / math.sqrt(length)
    tables = make_tables(doubled)
    own_skip = lax.dynamic_slice_in_dim(skip_gain, lax.axis_index("seq") * channels, channels)[
        :, None
    ]
    stacked = jnp.stack([query_proj, key_proj, value_proj])
    previous = passed_along(stacked[:, positions - 2 :], "seq", 1)
    extended = jnp.concatenate([previous, stacked], 1).astype(jnp.float32)
    tap_rows = short_taps[:, :, None, :]
    shorted = (
        tap_rows[:, 0] * extended[:, 2 : positions + 2]
        + tap_rows[:, 1] * extended[:, 1 : positions + 1]
        + tap_rows[:, 2] * extended[:, 0:positions]
    )
    shorted = shorted.astype(jnp.bfloat16)
    query_short, key_short, value_short = (shorted[0], shorted[1], shorted[2])
    key_wide = key_short.astype(jnp.float32)
    value_wide = value_short.astype(jnp.float32)
    product_in = (key_wide * value_wide).astype(jnp.bfloat16)
    kernel_own = long_filter * factor_root
    kernel_mirror = mirror_rows(kernel_own)
    zero_column = jnp.zeros((channels, 1), jnp.float32)
    kernel_full = jnp.concatenate(
        [
            kernel_own[:, :1] + kernel_mirror[:, :1],
            kernel_own[:, 1:],
            zero_column,
            kernel_mirror[:, 1:][:, ::-1],
        ],
        1,
    )
    spectrum_kernel = spectrum_of(kernel_full, tables)
    query_wide = query_short.astype(jnp.float32)
    chan_product = lax.all_to_all(product_in.T, "seq", split_axis=0, concat_axis=1, tiled=True)
    input_wide = chan_product.astype(jnp.float32)
    input_spectrum = spectrum_of(
        jnp.concatenate([input_wide, jnp.zeros_like(input_wide)], 1), tables
    )
    mixed_wide = signal_of(times_spec(spectrum_kernel, input_spectrum), tables)[:, :length]
    chan_mix, input_spectrum = (
        (mixed_wide + own_skip * input_wide).astype(jnp.bfloat16),
        input_spectrum,
    )
    long_mix = lax.all_to_all(chan_mix, "seq", split_axis=1, concat_axis=0, tiled=True).T
    gate_grad = (out_grad.astype(jnp.float32) * query_wide).astype(jnp.bfloat16)
    chan_gate = lax.all_to_all(gate_grad.T, "seq", split_axis=0, concat_axis=1, tiled=True)
    grad_wide = chan_gate.astype(jnp.float32)
    spectrum_grad = spectrum_of(jnp.concatenate([grad_wide, jnp.zeros_like(grad_wide)], 1), tables)
    back_wide = signal_of(conj_times(spectrum_kernel, spectrum_grad), tables)[:, :length]
    lagged = signal_of(conj_times(input_spectrum, spectrum_grad), tables)
    chan_back, lagged = ((back_wide + own_skip * grad_wide).astype(jnp.bfloat16), lagged)
    input_grad = lax.all_to_all(chan_back, "seq", split_axis=1, concat_axis=0, tiled=True).T
    mix_wide = long_mix.astype(jnp.float32)
    mixed_out = (query_wide * mix_wide).astype(jnp.bfloat16)
    reversed_part = jnp.concatenate([lagged[:, :1], lagged[:, length + 1 :][:, ::-1]], 1)
    filter_grad = (lagged[:, :length] + mirror_rows(reversed_part)) * factor_root
    input_back = input_grad.astype(jnp.float32)
    gated = jnp.stack(
        [out_grad.astype(jnp.float32) * mix_wide, input_back * value_wide, input_back * key_wide]
    )
    following = passed_along(gated[:, :2], "seq", -1)
    widened = jnp.concatenate([gated, following], 1)
    tap_grads = (
        tap_rows[:, 0] * widened[:, 0:positions]
        + tap_rows[:, 1] * widened[:, 1 : positions + 1]
        + tap_rows[:, 2] * widened[:, 2 : positions + 2]
    )
    tap_grads = tap_grads.astype(jnp.bfloat16)
    return (mixed_out, tap_grads[0], tap_grads[1], tap_grads[2], filter_grad)


def solution(mesh):
    in_specs = (
        P("seq", "chan"),
        P("seq", "chan"),
        P("seq", "chan"),
        P(None, None, "chan"),
        P("chan"),
        P(("chan", "seq"), None),
        P("seq", "chan"),
    )
    out_specs = (
        P("seq", "chan"),
        P("seq", "chan"),
        P("seq", "chan"),
        P("seq", "chan"),
        P(("chan", "seq"), None),
    )
    n_seq, n_chan = mesh.shape["seq"], mesh.shape["chan"]

    def on_device(query_proj, key_proj, value_proj, short_taps, skip_gain, long_filter, out_grad):
        arguments = (
            query_proj, key_proj, value_proj, short_taps, skip_gain, long_filter, out_grad
        )
        rows, width = query_proj.shape
        channels, length = long_filter.shape
        if (
            rows == channels == BLOCK
            and n_seq % 2 == 0
            and n_chan % 2 == 0
            and length <= 1024
        ):
            tables = transform_tables(length)
            return tuple(dense_device(n_seq, n_chan, tables, *arguments))
        return per_device(*arguments)

    return jax.shard_map(
        on_device, mesh=mesh, in_specs=in_specs, out_specs=out_specs, check_vma=False
    )
```

```python
import functools
import math

import jax
import jax.numpy as jnp
import ml_dtypes
import numpy as np
from jax import lax
from jax.experimental import pallas as pl
from jax.experimental.pallas import tpu as pltpu
from jax.sharding import PartitionSpec as P

F32 = jnp.float32
BF16 = jnp.bfloat16
BLOCK = 128


def transform_tables(length):
    odd = 2 * np.arange(length, dtype=np.int64) + 1
    counts = odd[:, None] * np.arange(length, dtype=np.int64)[None, :] % (4 * length)
    angles = counts * (math.pi / (2 * length))
    forward = np.concatenate([np.cos(angles), np.sin(angles)], 0)
    forward = forward.astype(ml_dtypes.bfloat16)
    return forward, np.ascontiguousarray(forward.T)


def dense_kernel(
    n_seq,
    n_chan,
    query_hbm,
    key_hbm,
    value_hbm,
    taps_ref,
    skip_ref,
    filter_hbm,
    cotangent_hbm,
    forward_hbm,
    inverse_hbm,
    mixed_hbm,
    query_grad_hbm,
    key_grad_hbm,
    value_grad_hbm,
    filter_grad_hbm,
    arguments,
    filter_ref,
    outputs,
    filter_grad_ref,
    forward,
    inverse,
    extended,
    shorted,
    gated,
    halo_out,
    halo_in,
    block_out,
    block_in,
    mix_out,
    back_out,
    mix_in,
    back_in,
    filter_out,
    filter_in,
    skip_in,
    terms_out,
    terms_in,
    spectra,
    products,
    even_part,
    odd_part,
    lag_spectra,
    kernel_spectra,
    halo_sent,
    halo_got,
    block_sent,
    block_got,
    result_sent,
    result_got,
    single_sent,
    single_got,
    table_got,
    argument_got,
    output_sent,
):
    rows = query_hbm.shape[0]
    length = filter_hbm.shape[1]
    chunk = 2 * rows
    chunks = length // chunk
    me = lax.axis_index("seq")
    chan = lax.axis_index("chan")
    is_owner = chan % 2 == 0
    not_owner = chan % 2 == 1
    owner_chan = jnp.where(is_owner, chan, n_chan - 1 - chan)
    other_chan = n_chan - 1 - owner_chan
    side = chan % 2
    mirrored_seq = n_seq - 1 - me

    def device(seq, chan_index):
        return {"seq": seq, "chan": chan_index}

    def remote(source, target, sent, got, where):
        return pltpu.make_async_remote_copy(
            src_ref=source,
            dst_ref=target,
            send_sem=sent,
            recv_sem=got,
            device_id=where,
            device_id_type=pl.DeviceIdType.MESH,
        )

    def await_on(buffer, semaphore):
        pltpu.make_async_copy(buffer, buffer, semaphore).wait()

    def lanes_of(block):
        return pl.ds(pl.multiple_of(block * BLOCK, BLOCK), BLOCK)

    forward_copy = pltpu.make_async_copy(forward_hbm, forward, table_got.at[0])
    inverse_copy = pltpu.make_async_copy(inverse_hbm, inverse, table_got.at[1])

    argument_copies = [
        pltpu.make_async_copy(source, arguments.at[p], argument_got.at[p])
        for p, source in enumerate((query_hbm, key_hbm, value_hbm, cotangent_hbm))
    ]
    filter_load = pltpu.make_async_copy(filter_hbm, filter_ref, argument_got.at[4])
    for copy in argument_copies:
        copy.start()
    filter_load.start()

    barrier = pltpu.get_barrier_semaphore()

    def greet(index, carry):
        seq = index % n_seq
        target = jnp.where(index < n_seq, owner_chan, other_chan)

        @pl.when(jnp.logical_or(seq != me, target != chan))
        def _():
            pl.semaphore_signal(
                barrier,
                inc=1,
                device_id=device(seq, target),
                device_id_type=pl.DeviceIdType.MESH,
            )

        return carry

    lax.fori_loop(0, 2 * n_seq, greet, 0)

    @pl.when(is_owner)
    def _():
        forward_copy.start()
        inverse_copy.start()

    for p in range(4):
        argument_copies[p].wait()
        extended[p, 8 : rows + 8, :] = arguments[p].astype(F32)
    halo_out[0] = jnp.concatenate([extended[p, rows + 6 : rows + 8, :] for p in range(4)], 0)
    halo_out[1] = jnp.concatenate([extended[p, 8:10, :] for p in range(4)], 0)

    pl.semaphore_wait(barrier, 2 * n_seq - 1)

    to_next = remote(
        halo_out.at[0],
        halo_in.at[0],
        halo_sent.at[0],
        halo_got.at[0],
        device(jnp.minimum(me + 1, n_seq - 1), chan),
    )
    to_previous = remote(
        halo_out.at[1],
        halo_in.at[1],
        halo_sent.at[1],
        halo_got.at[1],
        device(jnp.maximum(me - 1, 0), chan),
    )

    @pl.when(me < n_seq - 1)
    def _():
        to_next.start()

    @pl.when(me > 0)
    def _():
        to_previous.start()

    filter_copy = remote(
        filter_out,
        filter_in,
        single_sent.at[0],
        single_got.at[0],
        device(mirrored_seq, owner_chan),
    )
    skip_copy = remote(
        skip_ref, skip_in, single_sent.at[1], single_got.at[1], device(mirrored_seq, owner_chan)
    )
    terms_copy = remote(
        terms_out, terms_in, single_sent.at[2], single_got.at[2], device(mirrored_seq, other_chan)
    )

    @pl.when(not_owner)
    def _():
        skip_copy.start()
        filter_load.wait()
        filter_out[...] = filter_ref[...].astype(BF16)
        filter_copy.start()

    @pl.when(me > 0)
    def _():
        await_on(halo_in.at[0], halo_got.at[0])

    @pl.when(me == 0)
    def _():
        halo_in[0] = jnp.zeros(halo_in.shape[1:], F32)

    @pl.when(me < n_seq - 1)
    def _():
        await_on(halo_in.at[1], halo_got.at[1])

    @pl.when(me == n_seq - 1)
    def _():
        halo_in[1] = jnp.zeros(halo_in.shape[1:], F32)

    for p in range(4):
        extended[p, 6:8, :] = halo_in[0, 2 * p : 2 * p + 2, :]
        extended[p, rows + 8 : rows + 16, :] = jnp.concatenate(
            [halo_in[1, 2 * p : 2 * p + 2, :], jnp.zeros((6, halo_in.shape[2]), F32)], 0
        )

    def owner_of(block):
        return jnp.where(is_owner, block, n_seq - 1 - block)

    def shorten(p, lanes):
        total = taps_ref[p, 0:1, lanes] * extended[p, 8 : rows + 16, lanes]
        total += taps_ref[p, 1:2, lanes] * extended[p, 7 : rows + 15, lanes]
        total += taps_ref[p, 2:3, lanes] * extended[p, 6 : rows + 14, lanes]
        shorted[p, :, lanes] = total.astype(BF16).astype(F32)

    def send_block(kind, block):
        here = jnp.logical_and(is_owner, block == me)

        @pl.when(here)
        def _():
            pltpu.make_async_copy(
                block_out.at[kind, block], block_in.at[kind, 0, me], block_got.at[kind, 0, me]
            ).start()

        @pl.when(jnp.logical_not(here))
        def _():
            remote(
                block_out.at[kind, block],
                block_in.at[kind, side, me],
                block_sent.at[kind, block],
                block_got.at[kind, side, me],
                device(owner_of(block), owner_chan),
            ).start()

    def send_input(step, carry):
        block = (me + n_seq // 2 + step) % n_seq
        lanes = lanes_of(block)
        shorten(1, lanes)
        shorten(2, lanes)
        product = shorted[1, 0:rows, lanes] * shorted[2, 0:rows, lanes]
        block_out[0, block] = product.astype(BF16)
        send_block(0, block)
        return carry

    def send_gate(step, carry):
        block = (me + n_seq // 2 + step) % n_seq
        lanes = lanes_of(block)
        shorten(0, lanes)
        gate = extended[3, 8 : rows + 8, lanes] * shorted[0, 0:rows, lanes]
        block_out[1, block] = gate.astype(BF16)
        send_block(1, block)
        return carry

    lax.fori_loop(0, n_seq, send_input, 0)
    lax.fori_loop(0, n_seq, send_gate, 0)

    def columns_of(kind, seq):
        return jnp.concatenate([block_in[kind, 0, seq], block_in[kind, 1, seq]], 1)

    wide = 2 * BLOCK

    @pl.when(is_owner)
    def _():
        scale = 1.0 / (length * math.sqrt(length))
        down = lax.broadcasted_iota(jnp.int32, (BLOCK, BLOCK), 0)
        across = lax.broadcasted_iota(jnp.int32, (BLOCK, BLOCK), 1)
        flip = jnp.where(down + across == BLOCK - 1, 1.0, 0.0).astype(BF16)

        def flipped(values):
            return jnp.dot(flip, values, preferred_element_type=F32)

        def halves(index):
            start = pl.multiple_of(index * chunk, chunk)
            return pl.ds(start, chunk), pl.ds(length + start, chunk)

        forward_copy.wait()
        filter_load.wait()
        await_on(filter_in, single_got.at[0])
        own = filter_ref[...]
        other = filter_in[...]
        own_flipped = flipped(own.astype(BF16))
        other_flipped = flipped(other)
        other = other.astype(F32)
        even_part[0:BLOCK, :] = (own + other_flipped).astype(BF16)
        even_part[BLOCK:, :] = (other + own_flipped).astype(BF16)
        odd_part[0:BLOCK, :] = (own - other_flipped).astype(BF16)
        odd_part[BLOCK:, :] = (other - own_flipped).astype(BF16)

        def kernel_transform(index, carry):
            first, second = halves(index)
            contracted = (((1,), (1,)), ((), ()))
            kernel_spectra[first, :] = lax.dot_general(
                forward[first, :], even_part[...], contracted, preferred_element_type=F32
            )
            kernel_spectra[second, :] = lax.dot_general(
                forward[second, :], odd_part[...], contracted, preferred_element_type=F32
            )
            return carry

        lax.fori_loop(0, chunks, kernel_transform, 0)

        def transform_blocks(kind):
            lanes = slice(kind * wide, (kind + 1) * wide)
            for step in range(chunks):
                piece = (me // 2 + step) % chunks
                for half in range(2):
                    for from_side in range(2):
                        seq = 2 * piece + half
                        await_on(
                            block_in.at[kind, from_side, seq], block_got.at[kind, from_side, seq]
                        )
                columns = jnp.concatenate(
                    [columns_of(kind, 2 * piece), columns_of(kind, 2 * piece + 1)], 0
                )
                lags = pl.ds(pl.multiple_of(piece * chunk, chunk), chunk)

                def transform(index, carry):
                    at = pl.ds(pl.multiple_of(index * chunk, chunk), chunk)
                    term = jnp.dot(forward[at, lags], columns, preferred_element_type=F32)
                    if step == 0:
                        spectra[at, lanes] = term
                    else:
                        spectra[at, lanes] += term
                    return carry

                lax.fori_loop(0, 2 * chunks, transform, 0)

        def mix_products(index, carry):
            first, second = halves(index)
            kernel_cos, kernel_sin = kernel_spectra[first, :], kernel_spectra[second, :]
            input_cos, input_sin = spectra[first, 0:wide], spectra[second, 0:wide]
            mix_cos = kernel_cos * input_cos - kernel_sin * input_sin
            mix_sin = kernel_cos * input_sin + kernel_sin * input_cos
            products[first, 0:wide] = mix_cos.astype(BF16)
            products[second, 0:wide] = mix_sin.astype(BF16)
            return carry

        def back_products(index, carry):
            first, second = halves(index)
            kernel_cos, kernel_sin = kernel_spectra[first, :], kernel_spectra[second, :]
            grad_cos, grad_sin = spectra[first, wide:], spectra[second, wide:]
            back_cos = kernel_cos * grad_cos + kernel_sin * grad_sin
            back_sin = kernel_cos * grad_sin - kernel_sin * grad_cos
            products[first, wide:] = back_cos.astype(BF16)
            products[second, wide:] = back_sin.astype(BF16)
            return carry

        def send_result(kind, source, target, seq):
            remote(
                source.at[1, seq],
                target.at[mirrored_seq],
                result_sent.at[kind, 1, seq],
                result_got.at[kind, mirrored_seq],
                device(seq, other_chan),
            ).start()

            @pl.when(seq == me)
            def _():
                pltpu.make_async_copy(
                    source.at[0, me], target.at[me], result_got.at[kind, me]
                ).start()

            @pl.when(seq != me)
            def _():
                remote(
                    source.at[0, seq],
                    target.at[me],
                    result_sent.at[kind, 0, seq],
                    result_got.at[kind, me],
                    device(seq, owner_chan),
                ).start()

        first_piece = (me // 2 + chunks // 2) % chunks

        def sums_of(kind, index):
            at = pl.ds(pl.multiple_of(index * chunk, chunk), chunk)
            lanes = slice(kind * wide, (kind + 1) * wide)
            return jnp.dot(inverse[at, :], products[:, lanes], preferred_element_type=F32) * scale

        def mix_results(step, carry):
            index = (first_piece + chunks - step) % chunks
            sums = sums_of(0, index)
            for half in range(2):
                seq = 2 * index + half
                here = sums[half * rows : (half + 1) * rows]
                here = here + gains * columns_of(0, seq).astype(F32)
                mix_out[0, seq] = here[:, 0:BLOCK].astype(BF16)
                mix_out[1, seq] = here[:, BLOCK:].astype(BF16)
                send_result(0, mix_out, mix_in, seq)
            return carry

        def back_results(step, carry):
            index = (first_piece + chunks - step) % chunks
            sums = sums_of(1, index)
            for half in range(2):
                seq = 2 * index + half
                here = sums[half * rows : (half + 1) * rows]
                here = here + gains * columns_of(1, seq).astype(F32)
                before = (seq + n_seq - 1) % n_seq
                for to_side in range(2):
                    back = here[:, to_side * BLOCK : (to_side + 1) * BLOCK]
                    back_out[to_side, seq, 0:rows, :] = back.astype(BF16)
                    mix = mix_out[to_side, seq, 0:16, :].astype(F32)
                    edge = jnp.concatenate([mix[0:2], back[0:2], jnp.zeros((12, BLOCK), F32)], 0)

                    @pl.when(seq > 0)
                    def _():
                        back_out[to_side, before, rows:, :] = edge.astype(BF16)

            @pl.when(step > 0)
            def _():
                send_result(1, back_out, back_in, 2 * index + 1)

            send_result(1, back_out, back_in, 2 * index)
            return carry

        for to_side in range(2):
            back_out[to_side, n_seq - 1, rows:, :] = jnp.zeros((16, BLOCK), BF16)
        await_on(skip_in, single_got.at[1])
        gains = [skip_ref[pl.ds(me, 1), :], skip_in[pl.ds(mirrored_seq, 1), :]]
        gains = jnp.concatenate(gains, 1)
        transform_blocks(0)
        lax.fori_loop(0, chunks, mix_products, 0)
        inverse_copy.wait()
        lax.fori_loop(0, chunks, mix_results, 0)
        transform_blocks(1)
        lax.fori_loop(0, chunks, back_products, 0)
        lax.fori_loop(0, chunks, back_results, 0)
        send_result(1, back_out, back_in, 2 * first_piece + 1)

        def lag_products(index, carry):
            first, second = halves(index)
            input_cos, input_sin = spectra[first, 0:wide], spectra[second, 0:wide]
            grad_cos, grad_sin = spectra[first, wide:], spectra[second, wide:]
            real = input_cos * grad_cos + input_sin * grad_sin
            imag = input_sin * grad_cos - input_cos * grad_sin
            lag_spectra[:, first] = real.T.astype(BF16)
            lag_spectra[:, second] = imag.T.astype(BF16)
            return carry

        lax.fori_loop(0, chunks, lag_products, 0)
        def filter_terms(index, carry):
            lags = pl.ds(pl.multiple_of(index * chunk, chunk), chunk)
            cosine = jnp.dot(
                lag_spectra[:, 0:length], forward[0:length, lags], preferred_element_type=F32
            )
            sine = jnp.dot(
                lag_spectra[:, length:], forward[length:, lags], preferred_element_type=F32
            )
            ahead = cosine - sine
            behind = (cosine + sine).astype(BF16)
            terms_out[:, lags] = ((ahead[BLOCK:] + flipped(behind[:BLOCK])) * scale).astype(BF16)
            filter_grad_ref[:, lags] = (ahead[:BLOCK] + flipped(behind[BLOCK:])) * scale
            return carry

        lax.fori_loop(0, chunks, filter_terms, 0)
        terms_copy.start()

    targets = (mixed_hbm, query_grad_hbm, key_grad_hbm, value_grad_hbm)
    filter_store = pltpu.make_async_copy(filter_grad_ref, filter_grad_hbm, output_sent.at[4])

    @pl.when(is_owner)
    def _():
        filter_store.start()

    def store_block(p, lanes):
        pltpu.make_async_copy(
            outputs.at[p, :, lanes], targets[p].at[:, lanes], output_sent.at[p]
        ).start()

    def finish_mix(step, carry):
        block = owner_of((me + n_seq // 2 + step) % n_seq)
        lanes = lanes_of(block)
        await_on(mix_in.at[block], result_got.at[0, block])
        outputs[0, :, lanes] = (shorted[0, 0:rows, lanes] * mix_in[block].astype(F32)).astype(BF16)
        store_block(0, lanes)
        return carry

    def finish_block(step, carry):
        block = owner_of((me + n_seq // 2 + step) % n_seq)
        lanes = lanes_of(block)
        await_on(back_in.at[block], result_got.at[1, block])
        edge = back_in[block, rows:, :].astype(F32)
        spare = jnp.zeros((6, BLOCK), F32)
        mix = jnp.concatenate([mix_in[block].astype(F32), edge[0:2], spare], 0)
        back = jnp.concatenate([back_in[block, 0:rows, :].astype(F32), edge[2:4], spare], 0)
        gated[0] = extended[3, 8 : rows + 16, lanes] * mix
        gated[1] = back * shorted[2, :, lanes]
        gated[2] = back * shorted[1, :, lanes]
        for p in range(3):
            total = taps_ref[p, 0:1, lanes] * gated[p, 0:rows, :]
            total += taps_ref[p, 1:2, lanes] * gated[p, 1 : rows + 1, :]
            total += taps_ref[p, 2:3, lanes] * gated[p, 2 : rows + 2, :]
            outputs[p + 1, :, lanes] = total.astype(BF16)
            store_block(p + 1, lanes)
        return carry

    lax.fori_loop(0, n_seq, finish_mix, 0)
    lax.fori_loop(0, n_seq, finish_block, 0)

    @pl.when(not_owner)
    def _():
        await_on(terms_in, single_got.at[2])
        filter_grad_ref[...] = terms_in[...].astype(F32)
        filter_store.start()
        filter_copy.wait_send()
        skip_copy.wait_send()

    @pl.when(me < n_seq - 1)
    def _():
        to_next.wait_send()

    @pl.when(me > 0)
    def _():
        to_previous.wait_send()

    for p, target in enumerate(targets):
        pltpu.make_async_copy(outputs.at[p], target, output_sent.at[p]).wait()
    filter_store.wait()

    def drain_block(block, carry):
        @pl.when(jnp.logical_or(not_owner, block != me))
        def _():
            for kind in range(2):
                await_on(block_out.at[kind, block], block_sent.at[kind, block])

        return carry

    lax.fori_loop(0, n_seq, drain_block, 0)

    @pl.when(is_owner)
    def _():
        terms_copy.wait_send()

        def drain_result(seq, carry):
            for kind, source in enumerate((mix_out, back_out)):
                await_on(source.at[1, seq], result_sent.at[kind, 1, seq])

            @pl.when(seq != me)
            def _():
                for kind, source in enumerate((mix_out, back_out)):
                    await_on(source.at[0, seq], result_sent.at[kind, 0, seq])

            return carry

        lax.fori_loop(0, n_seq, drain_result, 0)


def hand_over(*refs):
    sources, targets, held = refs[:5], refs[5:10], refs[10:15]
    loaded, stored = refs[15], refs[16]
    loads = [
        pltpu.make_async_copy(sources[index], held[index], loaded.at[index]) for index in range(5)
    ]
    stores = [
        pltpu.make_async_copy(held[index], targets[index], stored.at[index]) for index in range(5)
    ]
    for load in loads:
        load.start()
    for load, store in zip(loads, stores):
        load.wait()
        store.start()
    for store in stores:
        store.wait()


def dense_device(
    n_seq, n_chan, tables, query, key, value, short_taps, skip_gain, long_filter, cotangent
):
    rows, width = query.shape
    channels, length = long_filter.shape
    whole = pl.BlockSpec(memory_space=pltpu.VMEM)
    apart = pl.BlockSpec(memory_space=pl.ANY)
    sequence_like = jax.ShapeDtypeStruct((rows, width), BF16)
    wide = 2 * channels
    semaphores = pltpu.SemaphoreType.DMA
    results = pl.pallas_call(
        functools.partial(dense_kernel, n_seq, n_chan),
        out_shape=(sequence_like,) * 4 + (jax.ShapeDtypeStruct((channels, length), F32),),
        in_specs=[apart] * 3 + [whole] * 2 + [apart] * 4,
        out_specs=(apart,) * 5,
        scratch_shapes=[
            pltpu.VMEM((4, rows, width), BF16),
            pltpu.VMEM((channels, length), F32),
            pltpu.VMEM((4, rows, width), BF16),
            pltpu.VMEM((channels, length), F32),
            pltpu.VMEM((2 * length, length), BF16),
            pltpu.VMEM((length, 2 * length), BF16),
            pltpu.VMEM((4, rows + 16, width), F32),
            pltpu.VMEM((3, rows + 8, width), F32),
            pltpu.VMEM((3, rows + 8, channels), F32),
            pltpu.VMEM((2, 8, width), F32),
            pltpu.VMEM((2, 8, width), F32),
            pltpu.VMEM((2, n_seq, rows, channels), BF16),
            pltpu.VMEM((2, 2, n_seq, rows, channels), BF16),
            pltpu.VMEM((2, n_seq, rows, channels), BF16),
            pltpu.VMEM((2, n_seq, rows + 16, channels), BF16),
            pltpu.VMEM((n_seq, rows, channels), BF16),
            pltpu.VMEM((n_seq, rows + 16, channels), BF16),
            pltpu.VMEM((channels, length), BF16),
            pltpu.VMEM((channels, length), BF16),
            pltpu.VMEM((n_seq, channels), F32),
            pltpu.VMEM((channels, length), BF16),
            pltpu.VMEM((channels, length), BF16),
            pltpu.VMEM((2 * length, 2 * wide), F32),
            pltpu.VMEM((2 * length, 2 * wide), BF16),
            pltpu.VMEM((wide, length), BF16),
            pltpu.VMEM((wide, length), BF16),
            pltpu.VMEM((wide, 2 * length), BF16),
            pltpu.VMEM((2 * length, wide), F32),
            semaphores((2,)),
            semaphores((2,)),
            semaphores((2, n_seq)),
            semaphores((2, 2, n_seq)),
            semaphores((2, 2, n_seq)),
            semaphores((2, n_seq)),
            semaphores((3,)),
            semaphores((3,)),
            semaphores((2,)),
            semaphores((5,)),
            semaphores((5,)),
        ],
        compiler_params=pltpu.CompilerParams(
            collective_id=0, has_side_effects=True, vmem_limit_bytes=56 * 1024 * 1024
        ),
    )(
        query,
        key,
        value,
        short_taps,
        skip_gain.reshape(n_seq, channels),
        long_filter,
        cotangent,
        *[jnp.asarray(table) for table in tables],
    )
    return pl.pallas_call(
        hand_over,
        out_shape=[jax.ShapeDtypeStruct(result.shape, result.dtype) for result in results],
        in_specs=[apart] * 5,
        out_specs=[apart] * 5,
        scratch_shapes=[pltpu.VMEM(result.shape, result.dtype) for result in results]
        + [semaphores((5,)), semaphores((5,))],
        compiler_params=pltpu.CompilerParams(vmem_limit_bytes=56 * 1024 * 1024),
    )(*results)


exact_mode = lax.Precision.HIGHEST


def from_partner(array, axis, stride):
    return lax.ppermute(array, axis, [(i, i ^ 1 << stride) for i in range(lax.axis_size(axis))])


def passed_along(array, axis, by):
    length = lax.axis_size(axis)
    pairs = [(i, i + by) for i in range(length) if 0 <= i + by < length]
    return lax.ppermute(array, axis, pairs)


def divisor_pair(total_size):
    first_side = 1
    for candidate in range(1, math.isqrt(total_size) + 1):
        if total_size % candidate == 0:
            first_side = candidate
    return (first_side, total_size // first_side)


def angle_table(height, across, period):
    counts = (
        jnp.arange(height, dtype=jnp.int32)[:, None]
        * jnp.arange(across, dtype=jnp.int32)[None, :]
        % period
    )
    angles = counts.astype(jnp.float32) * (2.0 * math.pi / period)
    return (jnp.cos(angles), jnp.sin(angles))


def make_tables(total_size):
    first_side, second_side = divisor_pair(total_size)
    return (
        angle_table(first_side, first_side, first_side),
        angle_table(first_side, second_side, total_size),
        angle_table(second_side, second_side, second_side),
        first_side,
        second_side,
    )


def right_product(values, matrix):
    return jnp.einsum("ckm,ml->ckl", values, matrix, precision=exact_mode)


def left_product(matrix, values):
    return jnp.einsum("kn,cnm->ckm", matrix, values, precision=exact_mode)


def spectrum_of(signal, tables):
    (
        (cos_first, sin_first),
        (cosine_rotation, sin_twist),
        (cos_second, sin_second),
        first_side,
        second_side,
    ) = tables
    shaped = signal.reshape(signal.shape[0], first_side, second_side)
    section_real = left_product(cos_first, shaped)
    section_imag = -left_product(sin_first, shaped)
    twist_real = section_real * cosine_rotation + section_imag * sin_twist
    twist_imag = section_imag * cosine_rotation - section_real * sin_twist
    return (
        right_product(twist_real, cos_second) + right_product(twist_imag, sin_second),
        right_product(twist_imag, cos_second) - right_product(twist_real, sin_second),
    )


def signal_of(spectrum, tables):
    (
        (cos_first, sin_first),
        (cosine_rotation, sin_twist),
        (cos_second, sin_second),
        first_side,
        second_side,
    ) = tables
    spec_real, spec_imag = spectrum
    section_real = right_product(spec_real, cos_second) - right_product(spec_imag, sin_second)
    section_imag = right_product(spec_imag, cos_second) + right_product(spec_real, sin_second)
    twist_real = section_real * cosine_rotation - section_imag * sin_twist
    twist_imag = section_imag * cosine_rotation + section_real * sin_twist
    result = left_product(cos_first, twist_real) - left_product(sin_first, twist_imag)
    return result.reshape(result.shape[0], -1) / (first_side * second_side)


def times_spec(former, latter):
    return (
        former[0] * latter[0] - former[1] * latter[1],
        former[0] * latter[1] + former[1] * latter[0],
    )


def conj_times(former, latter):
    return (
        former[0] * latter[0] + former[1] * latter[1],
        former[0] * latter[1] - former[1] * latter[0],
    )


def mirror_rows(block_rows):
    mirrored = block_rows
    for bit_index in range((lax.axis_size("seq") * lax.axis_size("chan")).bit_length() - 1):
        mirrored = from_partner(mirrored, ("seq", "chan"), bit_index)
    return mirrored[::-1]


def per_device(query_proj, key_proj, value_proj, short_taps, skip_gain, long_filter, out_grad):
    positions = query_proj.shape[0]
    channels, length = long_filter.shape
    doubled = 2 * length
    factor_root = 1.0 / math.sqrt(length)
    tables = make_tables(doubled)
    own_skip = lax.dynamic_slice_in_dim(skip_gain, lax.axis_index("seq") * channels, channels)[
        :, None
    ]
    stacked = jnp.stack([query_proj, key_proj, value_proj])
    previous = passed_along(stacked[:, positions - 2 :], "seq", 1)
    extended = jnp.concatenate([previous, stacked], 1).astype(jnp.float32)
    tap_rows = short_taps[:, :, None, :]
    shorted = (
        tap_rows[:, 0] * extended[:, 2 : positions + 2]
        + tap_rows[:, 1] * extended[:, 1 : positions + 1]
        + tap_rows[:, 2] * extended[:, 0:positions]
    )
    shorted = shorted.astype(jnp.bfloat16)
    query_short, key_short, value_short = (shorted[0], shorted[1], shorted[2])
    key_wide = key_short.astype(jnp.float32)
    value_wide = value_short.astype(jnp.float32)
    product_in = (key_wide * value_wide).astype(jnp.bfloat16)
    kernel_own = long_filter * factor_root
    kernel_mirror = mirror_rows(kernel_own)
    zero_column = jnp.zeros((channels, 1), jnp.float32)
    kernel_full = jnp.concatenate(
        [
            kernel_own[:, :1] + kernel_mirror[:, :1],
            kernel_own[:, 1:],
            zero_column,
            kernel_mirror[:, 1:][:, ::-1],
        ],
        1,
    )
    spectrum_kernel = spectrum_of(kernel_full, tables)
    query_wide = query_short.astype(jnp.float32)
    chan_product = lax.all_to_all(product_in.T, "seq", split_axis=0, concat_axis=1, tiled=True)
    input_wide = chan_product.astype(jnp.float32)
    input_spectrum = spectrum_of(
        jnp.concatenate([input_wide, jnp.zeros_like(input_wide)], 1), tables
    )
    mixed_wide = signal_of(times_spec(spectrum_kernel, input_spectrum), tables)[:, :length]
    chan_mix, input_spectrum = (
        (mixed_wide + own_skip * input_wide).astype(jnp.bfloat16),
        input_spectrum,
    )
    long_mix = lax.all_to_all(chan_mix, "seq", split_axis=1, concat_axis=0, tiled=True).T
    gate_grad = (out_grad.astype(jnp.float32) * query_wide).astype(jnp.bfloat16)
    chan_gate = lax.all_to_all(gate_grad.T, "seq", split_axis=0, concat_axis=1, tiled=True)
    grad_wide = chan_gate.astype(jnp.float32)
    spectrum_grad = spectrum_of(jnp.concatenate([grad_wide, jnp.zeros_like(grad_wide)], 1), tables)
    back_wide = signal_of(conj_times(spectrum_kernel, spectrum_grad), tables)[:, :length]
    lagged = signal_of(conj_times(input_spectrum, spectrum_grad), tables)
    chan_back, lagged = ((back_wide + own_skip * grad_wide).astype(jnp.bfloat16), lagged)
    input_grad = lax.all_to_all(chan_back, "seq", split_axis=1, concat_axis=0, tiled=True).T
    mix_wide = long_mix.astype(jnp.float32)
    mixed_out = (query_wide * mix_wide).astype(jnp.bfloat16)
    reversed_part = jnp.concatenate([lagged[:, :1], lagged[:, length + 1 :][:, ::-1]], 1)
    filter_grad = (lagged[:, :length] + mirror_rows(reversed_part)) * factor_root
    input_back = input_grad.astype(jnp.float32)
    gated = jnp.stack(
        [out_grad.astype(jnp.float32) * mix_wide, input_back * value_wide, input_back * key_wide]
    )
    following = passed_along(gated[:, :2], "seq", -1)
    widened = jnp.concatenate([gated, following], 1)
    tap_grads = (
        tap_rows[:, 0] * widened[:, 0:positions]
        + tap_rows[:, 1] * widened[:, 1 : positions + 1]
        + tap_rows[:, 2] * widened[:, 2 : positions + 2]
    )
    tap_grads = tap_grads.astype(jnp.bfloat16)
    return (mixed_out, tap_grads[0], tap_grads[1], tap_grads[2], filter_grad)


def solution(mesh):
    in_specs = (
        P("seq", "chan"),
        P("seq", "chan"),
        P("seq", "chan"),
        P(None, None, "chan"),
        P("chan"),
        P(("chan", "seq"), None),
        P("seq", "chan"),
    )
    out_specs = (
        P("seq", "chan"),
        P("seq", "chan"),
        P("seq", "chan"),
        P("seq", "chan"),
        P(("chan", "seq"), None),
    )
    n_seq, n_chan = mesh.shape["seq"], mesh.shape["chan"]

    def on_device(query_proj, key_proj, value_proj, short_taps, skip_gain, long_filter, out_grad):
        arguments = (
            query_proj, key_proj, value_proj, short_taps, skip_gain, long_filter, out_grad
        )
        rows, width = query_proj.shape
        channels, length = long_filter.shape
        if (
            rows == channels == BLOCK
            and n_seq % 2 == 0
            and n_chan % 2 == 0
            and length <= 1024
        ):
            tables = transform_tables(length)
            return tuple(dense_device(n_seq, n_chan, tables, *arguments))
        return per_device(*arguments)

    return jax.shard_map(
        on_device, mesh=mesh, in_specs=in_specs, out_specs=out_specs, check_vma=False
    )
```

```python
import functools
import math

import jax
import jax.numpy as jnp
import ml_dtypes
import numpy as np
from jax import lax
from jax.experimental import pallas as pl
from jax.experimental.pallas import tpu as pltpu
from jax.sharding import PartitionSpec as P

F32 = jnp.float32
BF16 = jnp.bfloat16
BLOCK = 128


def transform_tables(length):
    odd = 2 * np.arange(length, dtype=np.int64) + 1
    counts = odd[:, None] * np.arange(length, dtype=np.int64)[None, :] % (4 * length)
    angles = counts * (math.pi / (2 * length))
    forward = np.concatenate([np.cos(angles), np.sin(angles)], 0)
    forward = forward.astype(ml_dtypes.bfloat16)
    return forward, np.ascontiguousarray(forward.T)


def dense_kernel(
    n_seq,
    n_chan,
    query_hbm,
    key_hbm,
    value_hbm,
    taps_ref,
    skip_ref,
    filter_hbm,
    cotangent_hbm,
    forward_hbm,
    inverse_hbm,
    mixed_hbm,
    query_grad_hbm,
    key_grad_hbm,
    value_grad_hbm,
    filter_grad_hbm,
    arguments,
    filter_ref,
    outputs,
    filter_grad_ref,
    forward,
    inverse,
    extended,
    shorted,
    gated,
    halo_out,
    halo_in,
    block_out,
    block_in,
    result_out,
    result_in,
    filter_out,
    filter_in,
    skip_in,
    terms_out,
    terms_in,
    spectra,
    products,
    even_part,
    odd_part,
    lag_spectra,
    kernel_spectra,
    halo_sent,
    halo_got,
    block_sent,
    block_got,
    result_sent,
    result_got,
    single_sent,
    single_got,
    table_got,
    argument_got,
    output_sent,
    terms_sent,
    terms_got,
):
    rows = query_hbm.shape[0]
    length = filter_hbm.shape[1]
    chunk = 2 * rows
    chunks = length // chunk
    me = lax.axis_index("seq")
    chan = lax.axis_index("chan")
    is_owner = chan % 2 == 0
    not_owner = chan % 2 == 1
    owner_chan = jnp.where(is_owner, chan, n_chan - 1 - chan)
    other_chan = n_chan - 1 - owner_chan
    side = chan % 2
    mirrored_seq = n_seq - 1 - me

    def device(seq, chan_index):
        return {"seq": seq, "chan": chan_index}

    def remote(source, target, sent, got, where):
        return pltpu.make_async_remote_copy(
            src_ref=source,
            dst_ref=target,
            send_sem=sent,
            recv_sem=got,
            device_id=where,
            device_id_type=pl.DeviceIdType.MESH,
        )

    def await_on(buffer, semaphore):
        pltpu.make_async_copy(buffer, buffer, semaphore).wait()

    def lanes_of(block):
        return pl.ds(pl.multiple_of(block * BLOCK, BLOCK), BLOCK)

    forward_copy = pltpu.make_async_copy(forward_hbm, forward, table_got.at[0])
    inverse_copy = pltpu.make_async_copy(inverse_hbm, inverse, table_got.at[1])

    argument_copies = [
        pltpu.make_async_copy(source, arguments.at[p], argument_got.at[p])
        for p, source in enumerate((query_hbm, key_hbm, value_hbm, cotangent_hbm))
    ]
    filter_load = pltpu.make_async_copy(filter_hbm, filter_ref, argument_got.at[4])
    for copy in argument_copies:
        copy.start()
    filter_load.start()

    barrier = pltpu.get_barrier_semaphore()

    def greet(index, carry):
        seq = index % n_seq
        target = jnp.where(index < n_seq, owner_chan, other_chan)

        @pl.when(jnp.logical_or(seq != me, target != chan))
        def _():
            pl.semaphore_signal(
                barrier,
                inc=1,
                device_id=device(seq, target),
                device_id_type=pl.DeviceIdType.MESH,
            )

        return carry

    lax.fori_loop(0, 2 * n_seq, greet, 0)

    @pl.when(is_owner)
    def _():
        forward_copy.start()
        inverse_copy.start()

    for p in range(4):
        argument_copies[p].wait()
        extended[p, 8 : rows + 8, :] = arguments[p].astype(F32)
    halo_out[0] = jnp.concatenate([extended[p, rows + 6 : rows + 8, :] for p in range(4)], 0)
    halo_out[1] = jnp.concatenate([extended[p, 8:10, :] for p in range(4)], 0)

    pl.semaphore_wait(barrier, 2 * n_seq - 1)

    to_next = remote(
        halo_out.at[0],
        halo_in.at[0],
        halo_sent.at[0],
        halo_got.at[0],
        device(jnp.minimum(me + 1, n_seq - 1), chan),
    )
    to_previous = remote(
        halo_out.at[1],
        halo_in.at[1],
        halo_sent.at[1],
        halo_got.at[1],
        device(jnp.maximum(me - 1, 0), chan),
    )

    @pl.when(me < n_seq - 1)
    def _():
        to_next.start()

    @pl.when(me > 0)
    def _():
        to_previous.start()

    filter_copy = remote(
        filter_out,
        filter_in,
        single_sent.at[0],
        single_got.at[0],
        device(mirrored_seq, owner_chan),
    )
    skip_copy = remote(
        skip_ref, skip_in, single_sent.at[1], single_got.at[1], device(mirrored_seq, owner_chan)
    )

    def terms_copy(index):
        return remote(
            terms_out.at[index],
            terms_in.at[index],
            terms_sent.at[index],
            terms_got.at[index],
            device(mirrored_seq, other_chan),
        )

    @pl.when(not_owner)
    def _():
        skip_copy.start()
        filter_load.wait()
        filter_out[...] = filter_ref[...].astype(BF16)
        filter_copy.start()

    @pl.when(me > 0)
    def _():
        await_on(halo_in.at[0], halo_got.at[0])

    @pl.when(me == 0)
    def _():
        halo_in[0] = jnp.zeros(halo_in.shape[1:], F32)

    @pl.when(me < n_seq - 1)
    def _():
        await_on(halo_in.at[1], halo_got.at[1])

    @pl.when(me == n_seq - 1)
    def _():
        halo_in[1] = jnp.zeros(halo_in.shape[1:], F32)

    for p in range(4):
        extended[p, 6:8, :] = halo_in[0, 2 * p : 2 * p + 2, :]
        extended[p, rows + 8 : rows + 16, :] = jnp.concatenate(
            [halo_in[1, 2 * p : 2 * p + 2, :], jnp.zeros((6, halo_in.shape[2]), F32)], 0
        )

    def owner_of(block):
        return jnp.where(is_owner, block, n_seq - 1 - block)

    def send_block(step, carry):
        block = (me + n_seq // 2 + step) % n_seq
        lanes = lanes_of(block)
        for p in range(3):
            total = taps_ref[p, 0:1, lanes] * extended[p, 8 : rows + 16, lanes]
            total += taps_ref[p, 1:2, lanes] * extended[p, 7 : rows + 15, lanes]
            total += taps_ref[p, 2:3, lanes] * extended[p, 6 : rows + 14, lanes]
            shorted[p, :, lanes] = total.astype(BF16).astype(F32)
        product = shorted[1, 0:rows, lanes] * shorted[2, 0:rows, lanes]
        block_out[block, 0:rows, :] = product.astype(BF16)
        gate = extended[3, 8 : rows + 8, lanes] * shorted[0, 0:rows, lanes]
        block_out[block, rows : 2 * rows, :] = gate.astype(BF16)
        target = owner_of(block)
        here = jnp.logical_and(is_owner, block == me)

        @pl.when(here)
        def _():
            pltpu.make_async_copy(
                block_out.at[block], block_in.at[0, me], block_got.at[0, me]
            ).start()

        @pl.when(jnp.logical_not(here))
        def _():
            remote(
                block_out.at[block],
                block_in.at[side, me],
                block_sent.at[block],
                block_got.at[side, me],
                device(target, owner_chan),
            ).start()

        return carry

    lax.fori_loop(0, n_seq, send_block, 0)

    def columns_of(seq):
        return jnp.concatenate(
            [
                block_in[0, seq, 0:rows, :],
                block_in[1, seq, 0:rows, :],
                block_in[0, seq, rows : 2 * rows, :],
                block_in[1, seq, rows : 2 * rows, :],
            ],
            1,
        )

    wide = 2 * BLOCK

    @pl.when(is_owner)
    def _():
        scale = 1.0 / (length * math.sqrt(length))
        down = lax.broadcasted_iota(jnp.int32, (BLOCK, BLOCK), 0)
        across = lax.broadcasted_iota(jnp.int32, (BLOCK, BLOCK), 1)
        flip = jnp.where(down + across == BLOCK - 1, 1.0, 0.0).astype(BF16)

        def flipped(values):
            return jnp.dot(flip, values, preferred_element_type=F32)

        def halves(index):
            start = pl.multiple_of(index * chunk, chunk)
            return pl.ds(start, chunk), pl.ds(length + start, chunk)

        forward_copy.wait()
        filter_load.wait()
        await_on(filter_in, single_got.at[0])
        own = filter_ref[...]
        other = filter_in[...]
        own_flipped = flipped(own.astype(BF16))
        other_flipped = flipped(other)
        other = other.astype(F32)
        even_part[0:BLOCK, :] = (own + other_flipped).astype(BF16)
        even_part[BLOCK:, :] = (other + own_flipped).astype(BF16)
        odd_part[0:BLOCK, :] = (own - other_flipped).astype(BF16)
        odd_part[BLOCK:, :] = (other - own_flipped).astype(BF16)

        def kernel_transform(index, carry):
            first, second = halves(index)
            contracted = (((1,), (1,)), ((), ()))
            kernel_spectra[first, :] = lax.dot_general(
                forward[first, :], even_part[...], contracted, preferred_element_type=F32
            )
            kernel_spectra[second, :] = lax.dot_general(
                forward[second, :], odd_part[...], contracted, preferred_element_type=F32
            )
            return carry

        lax.fori_loop(0, chunks, kernel_transform, 0)

        for step in range(chunks):
            piece = (me // 2 + step) % chunks
            for half in range(2):
                for from_side in range(2):
                    seq = 2 * piece + half
                    await_on(block_in.at[from_side, seq], block_got.at[from_side, seq])
            columns = jnp.concatenate([columns_of(2 * piece), columns_of(2 * piece + 1)], 0)
            lags = pl.ds(pl.multiple_of(piece * chunk, chunk), chunk)

            def transform(index, carry):
                at = pl.ds(pl.multiple_of(index * chunk, chunk), chunk)
                term = jnp.dot(forward[at, lags], columns, preferred_element_type=F32)
                if step == 0:
                    spectra[at, :] = term
                else:
                    spectra[at, :] += term
                return carry

            lax.fori_loop(0, 2 * chunks, transform, 0)

        def spectral_products(index, carry):
            first, second = halves(index)
            kernel_cos, kernel_sin = kernel_spectra[first, :], kernel_spectra[second, :]
            input_cos, input_sin = spectra[first, 0:wide], spectra[second, 0:wide]
            grad_cos, grad_sin = spectra[first, wide:], spectra[second, wide:]
            mix_cos = kernel_cos * input_cos - kernel_sin * input_sin
            mix_sin = kernel_cos * input_sin + kernel_sin * input_cos
            back_cos = kernel_cos * grad_cos + kernel_sin * grad_sin
            back_sin = kernel_cos * grad_sin - kernel_sin * grad_cos
            products[first, 0:wide] = mix_cos.astype(BF16)
            products[second, 0:wide] = mix_sin.astype(BF16)
            products[first, wide:] = back_cos.astype(BF16)
            products[second, wide:] = back_sin.astype(BF16)
            return carry

        lax.fori_loop(0, chunks, spectral_products, 0)
        await_on(skip_in, single_got.at[1])
        gains = [skip_ref[pl.ds(me, 1), :], skip_in[pl.ds(mirrored_seq, 1), :]]
        gains = jnp.concatenate(gains + gains, 1)
        inverse_copy.wait()

        def send_result(seq):
            remote(
                result_out.at[1, seq],
                result_in.at[mirrored_seq],
                result_sent.at[1, seq],
                result_got.at[mirrored_seq],
                device(seq, other_chan),
            ).start()

            @pl.when(seq == me)
            def _():
                pltpu.make_async_copy(
                    result_out.at[0, me], result_in.at[me], result_got.at[me]
                ).start()

            @pl.when(seq != me)
            def _():
                remote(
                    result_out.at[0, seq],
                    result_in.at[me],
                    result_sent.at[0, seq],
                    result_got.at[me],
                    device(seq, owner_chan),
                ).start()

        first_piece = (me // 2 + chunks // 2) % chunks
        for to_side in range(2):
            result_out[to_side, n_seq - 1, 2 * rows :, :] = jnp.zeros((16, BLOCK), BF16)

        def results(step, carry):
            index = (first_piece + chunks - step) % chunks
            at = pl.ds(pl.multiple_of(index * chunk, chunk), chunk)
            sums = jnp.dot(inverse[at, :], products[...], preferred_element_type=F32) * scale
            for half in range(2):
                seq = 2 * index + half
                here = sums[half * rows : (half + 1) * rows]
                here = here + gains * columns_of(seq).astype(F32)
                before = (seq + n_seq - 1) % n_seq
                for to_side in range(2):
                    mix = here[:, to_side * BLOCK : (to_side + 1) * BLOCK]
                    back = here[:, wide + to_side * BLOCK : wide + (to_side + 1) * BLOCK]
                    result_out[to_side, seq, 0:rows, :] = mix.astype(BF16)
                    result_out[to_side, seq, rows : 2 * rows, :] = back.astype(BF16)
                    edge = jnp.concatenate([mix[0:2], back[0:2], jnp.zeros((12, BLOCK), F32)], 0)

                    @pl.when(seq > 0)
                    def _():
                        result_out[to_side, before, 2 * rows :, :] = edge.astype(BF16)

            @pl.when(step > 0)
            def _():
                send_result(2 * index + 1)

            send_result(2 * index)
            return carry

        lax.fori_loop(0, chunks, results, 0)
        send_result(2 * first_piece + 1)

        def lag_products(index, carry):
            first, second = halves(index)
            input_cos, input_sin = spectra[first, 0:wide], spectra[second, 0:wide]
            grad_cos, grad_sin = spectra[first, wide:], spectra[second, wide:]
            real = input_cos * grad_cos + input_sin * grad_sin
            imag = input_sin * grad_cos - input_cos * grad_sin
            lag_spectra[:, first] = real.T.astype(BF16)
            lag_spectra[:, second] = imag.T.astype(BF16)
            return carry

        lax.fori_loop(0, chunks, lag_products, 0)
        def filter_terms(index, carry):
            lags = pl.ds(pl.multiple_of(index * chunk, chunk), chunk)
            cosine = jnp.dot(
                lag_spectra[:, 0:length], forward[0:length, lags], preferred_element_type=F32
            )
            sine = jnp.dot(
                lag_spectra[:, length:], forward[length:, lags], preferred_element_type=F32
            )
            ahead = cosine - sine
            behind = (cosine + sine).astype(BF16)
            terms_out[index] = ((ahead[BLOCK:] + flipped(behind[:BLOCK])) * scale).astype(BF16)
            terms_copy(index).start()
            filter_grad_ref[:, lags] = (ahead[:BLOCK] + flipped(behind[BLOCK:])) * scale
            return carry

        lax.fori_loop(0, chunks, filter_terms, 0)

    targets = (mixed_hbm, query_grad_hbm, key_grad_hbm, value_grad_hbm)
    filter_store = pltpu.make_async_copy(filter_grad_ref, filter_grad_hbm, output_sent.at[4])

    @pl.when(is_owner)
    def _():
        filter_store.start()

    def finish_block(step, carry):
        source = (me + n_seq // 2 + step) % n_seq
        block = owner_of(source)
        lanes = lanes_of(block)
        await_on(result_in.at[block], result_got.at[block])
        edge = result_in[block, 2 * rows :, :].astype(F32)
        mix = result_in[block, 0:rows, :].astype(F32)
        back = result_in[block, rows : 2 * rows, :].astype(F32)
        spare = jnp.zeros((6, BLOCK), F32)
        outputs[0, :, lanes] = (shorted[0, 0:rows, lanes] * mix).astype(BF16)
        mix = jnp.concatenate([mix, edge[0:2], spare], 0)
        back = jnp.concatenate([back, edge[2:4], spare], 0)
        gated[0] = extended[3, 8 : rows + 16, lanes] * mix
        gated[1] = back * shorted[2, :, lanes]
        gated[2] = back * shorted[1, :, lanes]
        for p in range(3):
            total = taps_ref[p, 0:1, lanes] * gated[p, 0:rows, :]
            total += taps_ref[p, 1:2, lanes] * gated[p, 1 : rows + 1, :]
            total += taps_ref[p, 2:3, lanes] * gated[p, 2 : rows + 2, :]
            outputs[p + 1, :, lanes] = total.astype(BF16)
        for p, target in enumerate(targets):
            pltpu.make_async_copy(
                outputs.at[p, :, lanes], target.at[:, lanes], output_sent.at[p]
            ).start()
        return carry

    lax.fori_loop(0, n_seq, finish_block, 0)

    @pl.when(not_owner)
    def _():
        for index in range(chunks):
            lags = slice(index * chunk, (index + 1) * chunk)
            await_on(terms_in.at[index], terms_got.at[index])
            filter_grad_ref[:, lags] = terms_in[index].astype(F32)
        filter_store.start()
        filter_copy.wait_send()
        skip_copy.wait_send()

    @pl.when(me < n_seq - 1)
    def _():
        to_next.wait_send()

    @pl.when(me > 0)
    def _():
        to_previous.wait_send()

    for p, target in enumerate(targets):
        pltpu.make_async_copy(outputs.at[p], target, output_sent.at[p]).wait()
    filter_store.wait()

    def drain_block(block, carry):
        @pl.when(jnp.logical_or(not_owner, block != me))
        def _():
            await_on(block_out.at[block], block_sent.at[block])

        return carry

    lax.fori_loop(0, n_seq, drain_block, 0)

    @pl.when(is_owner)
    def _():
        for index in range(chunks):
            terms_copy(index).wait_send()

        def drain_result(seq, carry):
            await_on(result_out.at[1, seq], result_sent.at[1, seq])

            @pl.when(seq != me)
            def _():
                await_on(result_out.at[0, seq], result_sent.at[0, seq])

            return carry

        lax.fori_loop(0, n_seq, drain_result, 0)


def hand_over(*refs):
    sources, targets, held = refs[:5], refs[5:10], refs[10:15]
    loaded, stored = refs[15], refs[16]
    loads = [
        pltpu.make_async_copy(sources[index], held[index], loaded.at[index]) for index in range(5)
    ]
    stores = [
        pltpu.make_async_copy(held[index], targets[index], stored.at[index]) for index in range(5)
    ]
    for load in loads:
        load.start()
    for load, store in zip(loads, stores):
        load.wait()
        store.start()
    for store in stores:
        store.wait()


def dense_device(
    n_seq, n_chan, tables, query, key, value, short_taps, skip_gain, long_filter, cotangent
):
    rows, width = query.shape
    channels, length = long_filter.shape
    whole = pl.BlockSpec(memory_space=pltpu.VMEM)
    apart = pl.BlockSpec(memory_space=pl.ANY)
    sequence_like = jax.ShapeDtypeStruct((rows, width), BF16)
    wide = 2 * channels
    semaphores = pltpu.SemaphoreType.DMA
    results = pl.pallas_call(
        functools.partial(dense_kernel, n_seq, n_chan),
        out_shape=(sequence_like,) * 4 + (jax.ShapeDtypeStruct((channels, length), F32),),
        in_specs=[apart] * 3 + [whole] * 2 + [apart] * 4,
        out_specs=(apart,) * 5,
        scratch_shapes=[
            pltpu.VMEM((4, rows, width), BF16),
            pltpu.VMEM((channels, length), F32),
            pltpu.VMEM((4, rows, width), BF16),
            pltpu.VMEM((channels, length), F32),
            pltpu.VMEM((2 * length, length), BF16),
            pltpu.VMEM((length, 2 * length), BF16),
            pltpu.VMEM((4, rows + 16, width), F32),
            pltpu.VMEM((3, rows + 8, width), F32),
            pltpu.VMEM((3, rows + 8, channels), F32),
            pltpu.VMEM((2, 8, width), F32),
            pltpu.VMEM((2, 8, width), F32),
            pltpu.VMEM((n_seq, 2 * rows, channels), BF16),
            pltpu.VMEM((2, n_seq, 2 * rows, channels), BF16),
            pltpu.VMEM((2, n_seq, 2 * rows + 16, channels), BF16),
            pltpu.VMEM((n_seq, 2 * rows + 16, channels), BF16),
            pltpu.VMEM((channels, length), BF16),
            pltpu.VMEM((channels, length), BF16),
            pltpu.VMEM((n_seq, channels), F32),
            pltpu.VMEM((length // (2 * rows), channels, 2 * rows), BF16),
            pltpu.VMEM((length // (2 * rows), channels, 2 * rows), BF16),
            pltpu.VMEM((2 * length, 2 * wide), F32),
            pltpu.VMEM((2 * length, 2 * wide), BF16),
            pltpu.VMEM((wide, length), BF16),
            pltpu.VMEM((wide, length), BF16),
            pltpu.VMEM((wide, 2 * length), BF16),
            pltpu.VMEM((2 * length, wide), F32),
            semaphores((2,)),
            semaphores((2,)),
            semaphores((n_seq,)),
            semaphores((2, n_seq)),
            semaphores((2, n_seq)),
            semaphores((n_seq,)),
            semaphores((3,)),
            semaphores((3,)),
            semaphores((2,)),
            semaphores((5,)),
            semaphores((5,)),
            semaphores((length // (2 * rows),)),
            semaphores((length // (2 * rows),)),
        ],
        compiler_params=pltpu.CompilerParams(
            collective_id=0, has_side_effects=True, vmem_limit_bytes=56 * 1024 * 1024
        ),
    )(
        query,
        key,
        value,
        short_taps,
        skip_gain.reshape(n_seq, channels),
        long_filter,
        cotangent,
        *[jnp.asarray(table) for table in tables],
    )
    return pl.pallas_call(
        hand_over,
        out_shape=[jax.ShapeDtypeStruct(result.shape, result.dtype) for result in results],
        in_specs=[apart] * 5,
        out_specs=[apart] * 5,
        scratch_shapes=[pltpu.VMEM(result.shape, result.dtype) for result in results]
        + [semaphores((5,)), semaphores((5,))],
        compiler_params=pltpu.CompilerParams(vmem_limit_bytes=56 * 1024 * 1024),
    )(*results)


exact_mode = lax.Precision.HIGHEST


def from_partner(array, axis, stride):
    return lax.ppermute(array, axis, [(i, i ^ 1 << stride) for i in range(lax.axis_size(axis))])


def passed_along(array, axis, by):
    length = lax.axis_size(axis)
    pairs = [(i, i + by) for i in range(length) if 0 <= i + by < length]
    return lax.ppermute(array, axis, pairs)


def divisor_pair(total_size):
    first_side = 1
    for candidate in range(1, math.isqrt(total_size) + 1):
        if total_size % candidate == 0:
            first_side = candidate
    return (first_side, total_size // first_side)


def angle_table(height, across, period):
    counts = (
        jnp.arange(height, dtype=jnp.int32)[:, None]
        * jnp.arange(across, dtype=jnp.int32)[None, :]
        % period
    )
    angles = counts.astype(jnp.float32) * (2.0 * math.pi / period)
    return (jnp.cos(angles), jnp.sin(angles))


def make_tables(total_size):
    first_side, second_side = divisor_pair(total_size)
    return (
        angle_table(first_side, first_side, first_side),
        angle_table(first_side, second_side, total_size),
        angle_table(second_side, second_side, second_side),
        first_side,
        second_side,
    )


def right_product(values, matrix):
    return jnp.einsum("ckm,ml->ckl", values, matrix, precision=exact_mode)


def left_product(matrix, values):
    return jnp.einsum("kn,cnm->ckm", matrix, values, precision=exact_mode)


def spectrum_of(signal, tables):
    (
        (cos_first, sin_first),
        (cosine_rotation, sin_twist),
        (cos_second, sin_second),
        first_side,
        second_side,
    ) = tables
    shaped = signal.reshape(signal.shape[0], first_side, second_side)
    section_real = left_product(cos_first, shaped)
    section_imag = -left_product(sin_first, shaped)
    twist_real = section_real * cosine_rotation + section_imag * sin_twist
    twist_imag = section_imag * cosine_rotation - section_real * sin_twist
    return (
        right_product(twist_real, cos_second) + right_product(twist_imag, sin_second),
        right_product(twist_imag, cos_second) - right_product(twist_real, sin_second),
    )


def signal_of(spectrum, tables):
    (
        (cos_first, sin_first),
        (cosine_rotation, sin_twist),
        (cos_second, sin_second),
        first_side,
        second_side,
    ) = tables
    spec_real, spec_imag = spectrum
    section_real = right_product(spec_real, cos_second) - right_product(spec_imag, sin_second)
    section_imag = right_product(spec_imag, cos_second) + right_product(spec_real, sin_second)
    twist_real = section_real * cosine_rotation - section_imag * sin_twist
    twist_imag = section_imag * cosine_rotation + section_real * sin_twist
    result = left_product(cos_first, twist_real) - left_product(sin_first, twist_imag)
    return result.reshape(result.shape[0], -1) / (first_side * second_side)


def times_spec(former, latter):
    return (
        former[0] * latter[0] - former[1] * latter[1],
        former[0] * latter[1] + former[1] * latter[0],
    )


def conj_times(former, latter):
    return (
        former[0] * latter[0] + former[1] * latter[1],
        former[0] * latter[1] - former[1] * latter[0],
    )


def mirror_rows(block_rows):
    mirrored = block_rows
    for bit_index in range((lax.axis_size("seq") * lax.axis_size("chan")).bit_length() - 1):
        mirrored = from_partner(mirrored, ("seq", "chan"), bit_index)
    return mirrored[::-1]


def per_device(query_proj, key_proj, value_proj, short_taps, skip_gain, long_filter, out_grad):
    positions = query_proj.shape[0]
    channels, length = long_filter.shape
    doubled = 2 * length
    factor_root = 1.0 / math.sqrt(length)
    tables = make_tables(doubled)
    own_skip = lax.dynamic_slice_in_dim(skip_gain, lax.axis_index("seq") * channels, channels)[
        :, None
    ]
    stacked = jnp.stack([query_proj, key_proj, value_proj])
    previous = passed_along(stacked[:, positions - 2 :], "seq", 1)
    extended = jnp.concatenate([previous, stacked], 1).astype(jnp.float32)
    tap_rows = short_taps[:, :, None, :]
    shorted = (
        tap_rows[:, 0] * extended[:, 2 : positions + 2]
        + tap_rows[:, 1] * extended[:, 1 : positions + 1]
        + tap_rows[:, 2] * extended[:, 0:positions]
    )
    shorted = shorted.astype(jnp.bfloat16)
    query_short, key_short, value_short = (shorted[0], shorted[1], shorted[2])
    key_wide = key_short.astype(jnp.float32)
    value_wide = value_short.astype(jnp.float32)
    product_in = (key_wide * value_wide).astype(jnp.bfloat16)
    kernel_own = long_filter * factor_root
    kernel_mirror = mirror_rows(kernel_own)
    zero_column = jnp.zeros((channels, 1), jnp.float32)
    kernel_full = jnp.concatenate(
        [
            kernel_own[:, :1] + kernel_mirror[:, :1],
            kernel_own[:, 1:],
            zero_column,
            kernel_mirror[:, 1:][:, ::-1],
        ],
        1,
    )
    spectrum_kernel = spectrum_of(kernel_full, tables)
    query_wide = query_short.astype(jnp.float32)
    chan_product = lax.all_to_all(product_in.T, "seq", split_axis=0, concat_axis=1, tiled=True)
    input_wide = chan_product.astype(jnp.float32)
    input_spectrum = spectrum_of(
        jnp.concatenate([input_wide, jnp.zeros_like(input_wide)], 1), tables
    )
    mixed_wide = signal_of(times_spec(spectrum_kernel, input_spectrum), tables)[:, :length]
    chan_mix, input_spectrum = (
        (mixed_wide + own_skip * input_wide).astype(jnp.bfloat16),
        input_spectrum,
    )
    long_mix = lax.all_to_all(chan_mix, "seq", split_axis=1, concat_axis=0, tiled=True).T
    gate_grad = (out_grad.astype(jnp.float32) * query_wide).astype(jnp.bfloat16)
    chan_gate = lax.all_to_all(gate_grad.T, "seq", split_axis=0, concat_axis=1, tiled=True)
    grad_wide = chan_gate.astype(jnp.float32)
    spectrum_grad = spectrum_of(jnp.concatenate([grad_wide, jnp.zeros_like(grad_wide)], 1), tables)
    back_wide = signal_of(conj_times(spectrum_kernel, spectrum_grad), tables)[:, :length]
    lagged = signal_of(conj_times(input_spectrum, spectrum_grad), tables)
    chan_back, lagged = ((back_wide + own_skip * grad_wide).astype(jnp.bfloat16), lagged)
    input_grad = lax.all_to_all(chan_back, "seq", split_axis=1, concat_axis=0, tiled=True).T
    mix_wide = long_mix.astype(jnp.float32)
    mixed_out = (query_wide * mix_wide).astype(jnp.bfloat16)
    reversed_part = jnp.concatenate([lagged[:, :1], lagged[:, length + 1 :][:, ::-1]], 1)
    filter_grad = (lagged[:, :length] + mirror_rows(reversed_part)) * factor_root
    input_back = input_grad.astype(jnp.float32)
    gated = jnp.stack(
        [out_grad.astype(jnp.float32) * mix_wide, input_back * value_wide, input_back * key_wide]
    )
    following = passed_along(gated[:, :2], "seq", -1)
    widened = jnp.concatenate([gated, following], 1)
    tap_grads = (
        tap_rows[:, 0] * widened[:, 0:positions]
        + tap_rows[:, 1] * widened[:, 1 : positions + 1]
        + tap_rows[:, 2] * widened[:, 2 : positions + 2]
    )
    tap_grads = tap_grads.astype(jnp.bfloat16)
    return (mixed_out, tap_grads[0], tap_grads[1], tap_grads[2], filter_grad)


def solution(mesh):
    in_specs = (
        P("seq", "chan"),
        P("seq", "chan"),
        P("seq", "chan"),
        P(None, None, "chan"),
        P("chan"),
        P(("chan", "seq"), None),
        P("seq", "chan"),
    )
    out_specs = (
        P("seq", "chan"),
        P("seq", "chan"),
        P("seq", "chan"),
        P("seq", "chan"),
        P(("chan", "seq"), None),
    )
    n_seq, n_chan = mesh.shape["seq"], mesh.shape["chan"]

    def on_device(query_proj, key_proj, value_proj, short_taps, skip_gain, long_filter, out_grad):
        arguments = (
            query_proj, key_proj, value_proj, short_taps, skip_gain, long_filter, out_grad
        )
        rows, width = query_proj.shape
        channels, length = long_filter.shape
        if (
            rows == channels == BLOCK
            and n_seq % 2 == 0
            and n_chan % 2 == 0
            and length <= 1024
        ):
            tables = transform_tables(length)
            return tuple(dense_device(n_seq, n_chan, tables, *arguments))
        return per_device(*arguments)

    return jax.shard_map(
        on_device, mesh=mesh, in_specs=in_specs, out_specs=out_specs, check_vma=False
    )
```
